128 devices in a mesh: frames: 64 (over z, x_lo, y, core), bands: 2 (over x_hi).
Axes of the slice: x: 4 (x_hi: 2, x_lo: 2; x = x_hi * 2 + x_lo), y: 4, z: 4, core: 2. Of those that a mesh axis runs over, the one named last changes fastest.
Arguments:
- spectrum: bfloat16 [1, 4096, 1280], P(None, 'frames'), may hold values from -6 to 6
- band_widths: int32 [32], replicated, may hold values from 1 to 64, 640 in all
- band_weight: bfloat16 [32, 128, 384], P('bands'), may hold values from -0.5 to 0.5
- qkv_time: bfloat16 [384, 768], replicated
- out_time: bfloat16 [256, 384], replicated, may hold values from -0.375 to 0.375
- qkv_band: bfloat16 [384, 768], replicated
- out_band: bfloat16 [256, 384], replicated, may hold values from -0.375 to 0.375
- cotangent: bfloat16 [1, 32, 4096, 384], P(None, 'bands', 'frames'), may hold values from -0.059814453 to 0.059814453
Outputs:
- latent: bfloat16 [1, 32, 4096, 384], P(None, 'bands', 'frames')
- band_grad: float32 [32, 128, 384], P('bands')
- weight_grads: float32 [786432], P(('frames', 'bands'))
The draws below stay inside these ranges and needn't reach their ends.
Inputs may be any that keep to these rules, and one draw needn't show every extreme that they name: `band_widths`: the 32 band widths sum to 640 and one of them equals 64.
All inputs are finite; a program needn't handle non-finite values.
Results may differ from the reference program's by a relative error of at most 0.022.
Values may be sent and summed in bfloat16 or wider, within the bound.
A program may use at most 192 MiB of HBM per device.

```python
import math
import jax
import jax.numpy as jnp
import numpy as np
from jax import lax

D = 384
H = 4
HD = 64
INNER = 256
NB = 32
WMAX = 64
SPAN = 640
B = 1
FRAMES = 4096


def tied_projection(key):
    key_one, key_two, key_three = jax.random.split(key, 3)
    query_part = jax.random.normal(key_one, (D, INNER), jnp.float32)
    other_part = jax.random.normal(key_two, (D, INNER), jnp.float32)
    key_part = other_part
    value_part = jax.random.normal(key_three, (D, INNER), jnp.float32)
    return jnp.concatenate([query_part, key_part, value_part], axis=1) * D ** (-0.5)


def draw_qkv_time(key, part):
    key = jax.random.fold_in(key, 7)
    return tied_projection(key).astype(jnp.bfloat16)


def draw_qkv_band(key, part):
    key = jax.random.fold_in(key, 13)
    return tied_projection(key).astype(jnp.bfloat16)


def shard_levels(rng, dims, cuts, smallest, largest):
    loudness = 1.0
    for axis_at, shards_of in cuts:
        heights = jax.random.uniform(jax.random.fold_in(jax.random.fold_in(rng, 6), axis_at), (shards_of,), jnp.float32, smallest / len(cuts), largest / len(cuts))
        loudness = loudness * jnp.repeat(jnp.exp(heights), dims[axis_at] // shards_of).reshape((-1,) + (1,) * (len(dims) - 1 - axis_at))
    return loudness


def split_up(number_of, total, bound, slope):
    weights = [(1 << 20) // math.isqrt(standing ** slope) + 1 for standing in range(2, number_of + 1)]
    spare, holding = total - bound - (number_of - 1), [1] * (number_of - 1)
    while spare > 0:
        free = [i for i in range(number_of - 1) if holding[i] < bound]
        mass, remaining = sum([weights[i] for i in free]), spare
        for i in free:
            addition = min(bound - holding[i], max(1, remaining * weights[i] // mass), spare)
            holding[i] = holding[i] + addition
            spare = spare - addition
    return np.array([bound] + holding)


def uneven_parts(rng, number_of, total, most, skew):
    if number_of == 2:
        one = jax.random.randint(rng, (), max(1, total - most), min(most, total - 1) + 1)
        return jnp.stack([one, total - one])
    sizes = jnp.asarray(split_up(number_of, total, most, skew), jnp.int32)
    twos = (number_of - 1) // 2
    giver, sink = sizes[1:1 + 2 * twos:2], sizes[2:2 + 2 * twos:2]
    margin = jnp.minimum(giver - 1, most - sink)
    moved = jax.random.randint(jax.random.fold_in(rng, 1), (twos,), 0, 1 << 20) % (margin + 1)
    sizes = sizes.at[1:1 + 2 * twos:2].set(giver - moved).at[2:2 + 2 * twos:2].set(sink + moved)
    return sizes[jax.random.permutation(jax.random.fold_in(rng, 2), number_of)]


def normal_values(stream_key, extent, scale, limit, cuts=(), held_as=jnp.bfloat16):
    values = scale * jax.random.normal(stream_key, extent, jnp.float32)
    if cuts:
        values = values * shard_levels(stream_key, extent, cuts, -0.22, 0.18)
    return jnp.clip(values, -limit, limit).astype(held_as)


def setup_inputs(seed: int = 0) -> dict:
    arg_keys = jax.random.split(jax.random.key(seed), 9)
    return {
        "spectrum": normal_values(arg_keys[0], (B, FRAMES, 2 * SPAN), 1.0, 6.0, ((1, 64),)),
        "band_widths": uneven_parts(arg_keys[1], NB, SPAN, WMAX, 0).astype(jnp.int32),
        "band_weight": normal_values(arg_keys[2], (NB, 2 * WMAX, D), (2 * WMAX) ** -0.5, 0.5, ((0, 2),)),
        "qkv_time": draw_qkv_time(jax.random.fold_in(arg_keys[8], 71), 0),
        "out_time": normal_values(arg_keys[4], (INNER, D), INNER ** -0.5, 0.375),
        "qkv_band": draw_qkv_band(jax.random.fold_in(arg_keys[8], 71), 0),
        "out_band": normal_values(arg_keys[6], (INNER, D), INNER ** -0.5, 0.375),
        "cotangent": normal_values(arg_keys[7], (B, NB, FRAMES, D), 0.01, 0.059814453, ((1, 2), (2, 64))),
    }


EPS = 1e-05
THETA = 10000.0

def rms_norm(values):
    return values * lax.rsqrt(lax.optimization_barrier(jnp.mean(values * values, axis=-1, keepdims=True)) + EPS)

def lift(rounded):
    return lax.optimization_barrier(rounded).astype(jnp.float32)

def rotary_angles(positions, head_size):
    exponent = jnp.arange(head_size // 2, dtype=jnp.int32).astype(jnp.float32)
    frequency = jnp.exp(exponent * (-2.0 * math.log(THETA) / head_size))
    return positions.astype(jnp.float32)[:, None] * frequency[None, :]

def rotate(vectors, angles):
    half_size = vectors.shape[-1] // 2
    leading = vectors[..., :half_size]
    trailing = vectors[..., half_size:]
    cosine = jnp.cos(angles)
    sine_part = jnp.sin(angles)
    return jnp.concatenate([leading * cosine - trailing * sine_part, leading * sine_part + trailing * cosine], axis=-1)

def split_heads(values, n_heads):
    return values.reshape(values.shape[:-1] + (n_heads, values.shape[-1] // n_heads))

def merge_heads(values):
    return values.reshape(values.shape[:-2] + (values.shape[-2] * values.shape[-1],))

def band_features(spectrum, widths, first_band, band_count, feature_span):
    band_ends = jnp.cumsum(widths).astype(jnp.int32)
    starts = band_ends - widths
    own_starts = lax.dynamic_slice_in_dim(starts, first_band, band_count)
    own_widths = lax.dynamic_slice_in_dim(widths, first_band, band_count)
    offsets = jnp.arange(feature_span, dtype=jnp.int32)
    columns = (2 * own_starts[:, None] + offsets[None, :]).reshape(-1)
    padded = jnp.pad(spectrum, ((0, 0), (0, 0), (0, feature_span)))
    picked = jnp.take(padded, columns, axis=2)
    picked = picked.reshape(spectrum.shape[0], spectrum.shape[1], band_count, feature_span)
    keep_mask = offsets[None, :] < 2 * own_widths[:, None]
    return jnp.where(keep_mask, picked, jnp.zeros((), picked.dtype))

def project_bands(features, matrix):
    return jnp.einsum('btkj,kjd->bktd', features.astype(jnp.float32), matrix).astype(jnp.bfloat16)

def qkv_rotated(residual, matrix, angles, n_heads):
    inner_width = matrix.shape[1] // 3
    normed = rms_norm(residual).astype(jnp.bfloat16)
    projected = jnp.dot(lift(normed), matrix)
    query_part = rotate(split_heads(projected[..., :inner_width], n_heads), angles)
    key_part = rotate(split_heads(projected[..., inner_width:2 * inner_width], n_heads), angles)
    value_part = split_heads(projected[..., 2 * inner_width:], n_heads)
    return (query_part.astype(jnp.bfloat16), key_part.astype(jnp.bfloat16), value_part.astype(jnp.bfloat16))

def block_attend(q_block, keys_f, values_f):
    factor = q_block.shape[-1] ** (-0.5)
    scores = jnp.einsum('ntd,nsd->nts', lift(q_block), keys_f) * factor
    probs = lift(jax.nn.softmax(scores, axis=-1).astype(jnp.bfloat16))
    return jnp.einsum('nts,nsd->ntd', probs, values_f).astype(jnp.bfloat16)

def attention_items(queries, keys_in, values_in):
    n_items, n_time, head_size = queries.shape
    block = math.gcd(512, n_time)
    keys_f = lift(keys_in)
    values_f = lift(values_in)
    saved_attend = jax.checkpoint(block_attend)

    def one_block(q_block):
        return saved_attend(q_block, keys_f, values_f)
    blocks = queries.reshape(n_items, n_time // block, block, head_size).transpose(1, 0, 2, 3)
    result = lax.map(one_block, blocks)
    return result.transpose(1, 0, 2, 3).reshape(n_items, n_time, head_size)

def time_attention(queries, keys_in, values_in):

    def one_band(group):
        q_band, k_band, v_band = group
        n_batch, n_time, n_heads, head_size = q_band.shape

        def as_items(tensor):
            return tensor.transpose(0, 2, 1, 3).reshape(n_batch * n_heads, n_time, head_size)
        result = attention_items(as_items(q_band), as_items(k_band), as_items(v_band))
        return result.reshape(n_batch, n_heads, n_time, head_size).transpose(0, 2, 1, 3)
    moved = (jnp.moveaxis(queries, 1, 0), jnp.moveaxis(keys_in, 1, 0), jnp.moveaxis(values_in, 1, 0))
    return jnp.moveaxis(lax.map(one_band, moved), 0, 1)

def band_core(queries, keys_f, values_f, n_heads):
    head_size = queries.shape[-1] // n_heads
    q_heads = split_heads(lift(queries), n_heads)
    k_heads = split_heads(keys_f, n_heads)
    v_heads = split_heads(values_f, n_heads)
    scores = jnp.einsum('bqthd,bkthd->bthqk', q_heads, k_heads) * head_size ** (-0.5)
    probs = lift(jax.nn.softmax(scores, axis=-1).astype(jnp.bfloat16))
    attended = jnp.einsum('bthqk,bkthd->bqthd', probs, v_heads).astype(jnp.bfloat16)
    return attended.reshape(queries.shape)

def residual_out(residual, attended, out_matrix):
    return (residual + jnp.dot(lift(attended), out_matrix)).astype(jnp.bfloat16)

def forward(spectrum, band_widths, w_band, w_qkv_t, w_out_t, w_qkv_b, w_out_b):
    n_time = spectrum.shape[1]
    head_size = HD
    features = band_features(spectrum, band_widths, 0, NB, 2 * WMAX)
    residual = lift(project_bands(features, w_band))
    frame_angles = rotary_angles(jnp.arange(n_time, dtype=jnp.int32), head_size)
    t_query, t_key, t_value = qkv_rotated(residual, w_qkv_t, frame_angles[:, None, :], H)
    attended = merge_heads(time_attention(t_query, t_key, t_value))
    second_f = lift(residual_out(residual, attended, w_out_t))
    band_angles = rotary_angles(jnp.arange(NB, dtype=jnp.int32), head_size)
    b_query, b_key, b_value = qkv_rotated(second_f, w_qkv_b, band_angles[:, None, None, :], H)
    band_out = band_core(merge_heads(b_query), lift(merge_heads(b_key)), lift(merge_heads(b_value)), H)
    return residual_out(second_f, band_out, w_out_b)

def reference(spectrum, band_widths, band_weight, qkv_time, out_time, qkv_band, out_band, cotangent):
    matrices = tuple((matrix.astype(jnp.float32) for matrix in (band_weight, qkv_time, out_time, qkv_band, out_band)))

    def run_layers(w_band, w_qkv_t, w_out_t, w_qkv_b, w_out_b):
        return forward(spectrum, band_widths, w_band, w_qkv_t, w_out_t, w_qkv_b, w_out_b)
    latent, pullback = jax.vjp(run_layers, matrices[0], matrices[1], matrices[2], matrices[3], matrices[4])
    grads = pullback(cotangent)
    flat = jnp.concatenate([grad_part.reshape(-1) for grad_part in grads[1:]])
    return (latent, grads[0], flat)
```

```python
import math

import jax
import jax.numpy as jnp
import numpy as np
from jax import lax
from jax.experimental import pallas as pl
from jax.experimental.pallas import tpu as pltpu
from jax.sharding import PartitionSpec as P

EPS = 1e-05
THETA = 10000.0
NB = 32
NG = 16
NF = 64
ND = 128
FB = 64
HF = 32
T = 4096
D = 384
W = 128
BQ = 256
NQ = T // BQ
SAFE = 100.0 * 100.0
LOG2E = math.log2(math.e)
BF = jnp.bfloat16
F32 = jnp.float32
MESH = pl.DeviceIdType.MESH
VMEM_LIMIT = 60 * 1024 * 1024

NN = (((1,), (0,)), ((), ()))
NT = (((1,), (1,)), ((), ()))
TN = (((0,), (0,)), ((), ()))


def mm(a, b, dims=NN):
    return lax.dot_general(a, b, dims, preferred_element_type=F32)


def lanes(shape):
    return lax.broadcasted_iota(jnp.int32, shape, len(shape) - 1)


def swap_halves(x):
    lane = lanes(x.shape)
    ax = len(x.shape) - 1
    return jnp.where(lane % 64 < 32, pltpu.roll(x, 96, ax), pltpu.roll(x, 32, ax))


def rotary_tables(positions):
    i = np.arange(128) % 32
    freq = np.exp(i.astype(np.float64) * (-2.0 * math.log(THETA) / 64))
    sign = np.where(np.arange(128) % 64 < 32, -1.0, 1.0)
    ang = np.asarray(positions, np.float64)[:, None] * freq[None, :]
    return np.cos(ang).astype(np.float32), (np.sin(ang) * sign).astype(np.float32)


def prep_kernel(widths, spec, bw, feat, keep, send):
    bi = lax.axis_index("bands")
    start = jnp.int32(0)
    for j in range(NG):
        start = start + jnp.where(bi == 1, widths[j], 0)

    def one(k, start):
        w = widths[bi * NG + k]
        off = 2 * start
        blk = off // 128
        shift = off - blk * 128
        nxt = jnp.minimum(blk + 1, spec.shape[1] // 128 - 1)
        a = spec[:, pl.ds(pl.multiple_of(blk * 128, 128), 128)]
        b = spec[:, pl.ds(pl.multiple_of(nxt * 128, 128), 128)]
        x = jnp.concatenate([a, b], axis=1).astype(F32)
        y = pltpu.roll(x, lax.rem(256 - shift, 256), 1)[:, :128]
        y = jnp.where(lanes(y.shape) < 2 * w, y, 0.0).astype(BF)
        feat[k] = y
        lat = mm(y, bw[k]).astype(BF)

        @pl.when(bi == 0)
        def _():
            keep[k] = lat[:HF]
            send[k] = lat[HF:]

        @pl.when(bi == 1)
        def _():
            keep[k] = lat[HF:]
            send[k] = lat[:HF]

        return start + w

    lax.fori_loop(0, NG, one, start)


def angles_at(c, cc, sc, cr, sr):
    ca = cc[pl.ds(c, 1), :]
    sa = sc[pl.ds(c, 1), :]
    return ca * cr[...] - sa * sr[...], sa * cr[...] + ca * sr[...]


def normed_rows(feat_rows, bwk):
    lat = mm(feat_rows, bwk).astype(BF).astype(F32)
    r = lax.rsqrt(jnp.mean(lat * lat, axis=-1, keepdims=True) + EPS)
    return lat * r, r


def fwd_kernel(feat, bw, wh, cc, sc, cr, sr, e_out, q_out, k_out, v_out, ol_out, op_out, top):
    c = pl.program_id(0)
    band = lax.axis_index("frames") // 4

    @pl.when(c == 0)
    def _():
        top[...] = jnp.zeros_like(top)
        bwk = bw[band]

        def pre(j, _):
            rows = pl.ds(pl.multiple_of(j * BQ, BQ), BQ)
            n, _r = normed_rows(feat[rows, :], bwk)
            proj = mm(n.astype(BF), wh[...])
            co, si = angles_at(j, cc, sc, cr, sr)
            a = proj[:, :128]
            a = a * co + swap_halves(a) * si
            lane = lanes(a.shape)
            q = (a * jnp.where(lane < 64, 0.125 * LOG2E, 1.0)).astype(BF)
            qf = q.astype(F32)
            sq = qf * qf
            qn = jnp.max(jnp.sum(jnp.where(lane < 64, sq, 0.0), axis=1, keepdims=True))
            kn = jnp.max(jnp.sum(jnp.where(lane < 64, 0.0, sq), axis=1, keepdims=True))
            top[0:1, :] = jnp.maximum(top[0:1, :], qn)
            top[1:2, :] = jnp.maximum(top[1:2, :], kn)
            q_out[rows, :] = q
            k_out[rows, :] = jnp.where(lane < 64, pltpu.roll(qf, 64, 1), 0.0).astype(BF)
            v = jnp.concatenate([proj[:, 128:192], jnp.ones((BQ, 64), F32)], axis=1)
            v_out[rows, :] = v.astype(BF)
            return 0

        lax.fori_loop(0, NQ, pre, 0)

    rows = pl.ds(pl.multiple_of(c * BQ, BQ), BQ)
    q = q_out[rows, :]
    safe = jnp.max(top[0:1, :] * top[1:2, :]) < SAFE

    def finish(res):
        rl = 1.0 / res
        lane = lanes(res.shape)
        o = res * pltpu.roll(rl, 64, 1)
        ol_out[...] = jnp.where(lane < 64, o, rl)
        o4 = o.reshape(BQ // HF, 2, 16, 128)
        lane3 = lanes((BQ // HF, 16, 128))
        op_out[...] = jnp.where(lane3 < 64, o4[:, 0], pltpu.roll(o4[:, 1], 64, 2)).astype(BF)

    @pl.when(safe)
    def _():
        res = jnp.zeros((BQ, 128), F32)
        for j in range(8):
            cols = slice(j * 512, (j + 1) * 512)
            e = jnp.exp2(mm(q, k_out[cols, :], NT)).astype(BF)
            e_out[:, cols] = e
            res = res + mm(e, v_out[cols, :])
        finish(res)

    @pl.when(jnp.logical_not(safe))
    def _():
        s = mm(q, k_out[...], NT)
        e = jnp.exp2(s - jnp.max(s, axis=1, keepdims=True)).astype(BF)
        e_out[...] = e
        finish(mm(e, v_out[...]))


def bwd_kernel(e_in, feat, bw, wh, cc, sc, cr, sr, q_in, k_in, v_in, ol_in, dop, dsec, wrecv,
               gband, gq, wsum, dq_s, t_s, gb_s, gq_s):
    c = pl.program_id(0)
    fi = lax.axis_index("frames")
    rows = pl.ds(pl.multiple_of(c * BQ, BQ), BQ)

    @pl.when(c == 0)
    def _():
        t_s[...] = jnp.zeros_like(t_s)
        wsum[...] = jnp.sum(wrecv[...].astype(F32), axis=0)

    x = dop[...].astype(F32)
    do = jnp.concatenate([x[:, None], pltpu.roll(x, 64, 2)[:, None]], axis=1).reshape(BQ, 128)
    ol = ol_in[...]
    lane = lanes((BQ, 128))
    do = jnp.where(lane < 64, do * pltpu.roll(ol, 64, 1), 0.0)
    delta = jnp.sum(do * ol, axis=1, keepdims=True)
    hi = delta.astype(BF).astype(F32)
    aug = jnp.where(lane == 64, -hi, jnp.where(lane == 65, hi - delta, do)).astype(BF)
    do_t = do.T[:64].astype(BF)
    q_t = q_in[rows, :].astype(F32).T[:64].astype(BF)
    dq = jnp.zeros((BQ, 128), F32)
    for j in range(8):
        cols = slice(j * 512, (j + 1) * 512)
        e = e_in[:, cols]
        ds = (e.astype(F32) * mm(aug, v_in[cols, :], NT)).astype(BF)
        dq = dq + mm(ds, k_in[cols, :])
        t_s[0:64, cols] += mm(do_t, e)
        t_s[64:128, cols] += mm(q_t, ds)
    dq_s[rows, :] = dq * 0.125

    @pl.when(c == NQ - 1)
    def _():
        bwk = bw[fi // 4]
        gq_s[...] = jnp.zeros_like(gq_s)
        quarter = pl.ds(pl.multiple_of(lax.rem(fi, 4) * 1024, 1024), 1024)
        gb_s[...] = mm(feat[quarter, :], dsec[...], TN)

        def post(j, _):
            rows = pl.ds(pl.multiple_of(j * BQ, BQ), BQ)
            tx = t_s[:, rows].T
            a = jnp.where(lane < 64, dq_s[rows, :], tx * math.log(2.0)).astype(BF).astype(F32)
            co, si = angles_at(j, cc, sc, cr, sr)
            a = a * co - swap_halves(a) * si
            dproj = jnp.concatenate([a, tx[:, :64]], axis=1).astype(BF)
            dn = mm(dproj, wh[...], NT).astype(BF).astype(F32)
            f = feat[rows, :]
            n, r = normed_rows(f, bwk)
            dlat = (r * (dn - n * jnp.mean(n * dn, axis=1, keepdims=True))).astype(BF)
            gb_s[...] += mm(f, dlat, TN)
            gq_s[...] += mm(n.astype(BF), dproj, TN)
            return 0

        lax.fori_loop(0, NQ, post, 0)
        gband[...] = gb_s[...].reshape(4, 32, D).astype(BF)
        g = gq_s[...]
        g = jnp.concatenate([g, jnp.zeros((D, 64), F32)], axis=1)
        gq[...] = jnp.concatenate(
            [g[:, :128].reshape(48, 8, 128), g[:, 128:].reshape(48, 8, 128)], axis=1
        ).astype(BF)


def band_kernel(lat_own, lat_oth, cot_own, cot_oth, att, w_ot, w_qb, w_ob, cb, sb,
                lat_keep, lat_send, dsec_out, dop_out, wg_out,
                lat_s, cot_s, att_s, do_s, g_ot, g_qb, g_ob):
    bi = lax.axis_index("bands")
    own = pl.ds(pl.multiple_of(bi * 128, 128), 128)
    oth = pl.ds(pl.multiple_of((1 - bi) * 128, 128), 128)
    for ref, scr, where in ((lat_own, lat_s, own), (lat_oth, lat_s, oth), (cot_own, cot_s, own), (cot_oth, cot_s, oth)):
        x = ref[...].astype(F32)
        for g in range(4):
            scr[g, where, :] = x[:, 8 * g:8 * g + 8, :].reshape(128, D)
    lane = lanes((256, 128))
    low = lane < 64

    def pair(a, b, p):
        if p == 0:
            return jnp.where(low, a, pltpu.roll(b, 64, 1))
        return jnp.where(low, pltpu.roll(a, 64, 1), b)

    for j in range(2):
        x0 = att[:, 2 * j].astype(F32)
        x1 = att[:, 2 * j + 1].astype(F32)
        for g in range(4):
            p, rr = g // 2, g % 2
            a = x0[:, 8 * rr:8 * rr + 8, :].reshape(256, 128)
            b = x1[:, 8 * rr:8 * rr + 8, :].reshape(256, 128)
            att_s[g, :, 128 * j:128 * j + 128] = pair(a, b, p).astype(BF)

    g_ot[...] = jnp.zeros_like(g_ot)
    g_qb[...] = jnp.zeros_like(g_qb)
    g_ob[...] = jnp.zeros_like(g_ob)

    def group(g, _):
        att_g = att_s[g]
        cot = cot_s[g]
        cot_b = cot.astype(BF)
        sec = (lat_s[g] + mm(att_g, w_ot[...])).astype(BF).astype(F32)
        r = lax.rsqrt(jnp.mean(sec * sec, axis=-1, keepdims=True) + EPS)
        n = sec * r
        nb = n.astype(BF)
        proj = mm(nb, w_qb[...])
        dbatt = mm(cot_b, w_ob[...], NT)
        co, si = cb[...], sb[...]
        row_t = lax.broadcasted_iota(jnp.int32, (256, 256), 0) % 8
        col_t = lax.broadcasted_iota(jnp.int32, (256, 256), 1) % 8
        same = row_t == col_t
        batts, dqs, dks, dvs = [], [], [], []
        for j in range(2):
            q = proj[:, 128 * j:128 * j + 128]
            k = proj[:, 256 + 128 * j:384 + 128 * j]
            v = proj[:, 512 + 128 * j:640 + 128 * j].astype(BF)
            q = ((q * co + swap_halves(q) * si) * 0.125).astype(BF)
            k = (k * co + swap_halves(k) * si).astype(BF)
            do = dbatt[:, 128 * j:128 * j + 128].astype(BF)
            outs = []
            for hh in range(2):
                here = low if hh == 0 else jnp.logical_not(low)
                zero = jnp.zeros((), BF)
                qm = jnp.where(here, q, zero)
                dm = jnp.where(here, do, zero)
                s = jnp.where(same, mm(qm, k, NT), -jnp.inf)
                e = jnp.exp(s - jnp.max(s, axis=1, keepdims=True))
                p = e * (1.0 / jnp.sum(e, axis=1, keepdims=True))
                pb = p.astype(BF)
                pf = pb.astype(F32)
                o = mm(pb, v)
                dp = mm(dm, v, NT)
                ds = (pf * (dp - jnp.sum(pf * dp, axis=1, keepdims=True))).astype(BF)
                outs.append((o, mm(ds, k), mm(ds, q, TN), mm(pb, do, TN)))
            batts.append(jnp.where(low, outs[0][0], outs[1][0]).astype(BF))
            dq = (jnp.where(low, outs[0][1], outs[1][1]) * 0.125).astype(BF).astype(F32)
            dk = jnp.where(low, outs[0][2], outs[1][2]).astype(BF).astype(F32)
            dqs.append((dq * co - swap_halves(dq) * si).astype(BF))
            dks.append((dk * co - swap_halves(dk) * si).astype(BF))
            dvs.append(jnp.where(low, outs[0][3], outs[1][3]).astype(BF))
        batt = jnp.concatenate(batts, axis=1)
        dproj = jnp.concatenate(dqs + dks + dvs, axis=1)
        lat_s[g] = sec + mm(batt, w_ob[...])
        dn = mm(dproj, w_qb[...], NT).astype(BF).astype(F32)
        dsec = (cot + r * (dn - n * jnp.mean(n * dn, axis=1, keepdims=True))).astype(BF)
        cot_s[g] = dsec.astype(F32)
        do_s[g] = mm(dsec, w_ot[...], NT)
        g_ob[...] += mm(batt, cot_b, TN)
        g_qb[...] += mm(nb, dproj, TN)
        g_ot[...] += mm(att_g, dsec, TN)
        return 0

    lax.fori_loop(0, 4, group, 0)

    for ref, where in ((lat_keep, own), (lat_send, oth)):
        ref[...] = jnp.concatenate(
            [lat_s[g, where, :].reshape(NG, 8, D) for g in range(4)], axis=1
        ).astype(BF)
    dsec_out[...] = jnp.concatenate(
        [cot_s[g].reshape(NB, 8, D) for g in range(4)], axis=1
    ).astype(BF)
    for j in range(2):
        for hh in range(2):
            parts = []
            for rr in range(2):
                a = do_s[rr, :, 128 * j:128 * j + 128]
                b = do_s[2 + rr, :, 128 * j:128 * j + 128]
                parts.append(pair(a, b, hh).reshape(NB, 8, 128))
            dop_out[:, 2 * j + hh] = jnp.concatenate(parts, axis=1).astype(BF)
    wg_out[0:16] = g_ot[...].reshape(16, 16, D).astype(BF)
    wg_out[16:64] = jnp.concatenate(
        [g_qb[:, :D].reshape(48, 8, D), g_qb[:, D:].reshape(48, 8, D)], axis=1
    ).astype(BF)
    wg_out[64:80] = g_ob[...].reshape(16, 16, D).astype(BF)


def here():
    return lax.axis_index("frames"), lax.axis_index("bands")


def group_barrier():
    fi, bi = here()
    sem = pltpu.get_barrier_semaphore()

    def body(d, _):
        pl.semaphore_signal(sem, inc=1, device_id=(lax.rem(fi + d, NF), bi), device_id_type=MESH)
        return 0

    lax.fori_loop(1, NF, body, 0)
    pl.semaphore_wait(sem, NF - 1)


def full_barrier():
    fi, bi = here()
    me = fi * 2 + bi
    sem = pltpu.get_barrier_semaphore()

    def body(d, _):
        t = lax.rem(me + d, ND)
        pl.semaphore_signal(sem, inc=1, device_id=(t // 2, lax.rem(t, 2)), device_id_type=MESH)
        return 0

    lax.fori_loop(1, ND, body, 0)
    pl.semaphore_wait(sem, ND - 1)


def wait_bytes(ref, sem):
    pltpu.make_async_copy(ref, ref, sem).wait()


def send_feat_kernel(src, dst, send_sem, recv_sem):
    fi, bi = here()
    group_barrier()
    pltpu.make_async_copy(src.at[fi // 4], dst.at[fi], recv_sem).start()

    def body(d, _):
        t = lax.rem(fi + d, NF)
        pltpu.make_async_remote_copy(
            src.at[t // 4], dst.at[fi], send_sem, recv_sem, device_id=(t, bi), device_id_type=MESH
        ).start()
        return 0

    lax.fori_loop(1, NF, body, 0)
    wait_bytes(dst, recv_sem)
    wait_bytes(dst.at[pl.ds(0, NF - 1)], send_sem)


def send_att_kernel(src, dst, send_sem, recv_sem):
    fi, bi = here()
    me = fi * 2 + bi
    slot = bi * NF + fi
    full_barrier()
    pltpu.make_async_copy(src.at[me], dst.at[slot], recv_sem).start()

    def body(d, _):
        t = lax.rem(me + d, ND)
        pltpu.make_async_remote_copy(
            src.at[t], dst.at[slot], send_sem, recv_sem,
            device_id=(t // 2, lax.rem(t, 2)), device_id_type=MESH,
        ).start()
        return 0

    lax.fori_loop(1, ND, body, 0)
    wait_bytes(dst, recv_sem)
    wait_bytes(dst.at[pl.ds(0, ND - 1)], send_sem)


def send_back_kernel(dop, dsec, wg, dop_r, dsec_r, wg_r, send_sems, recv_sems):
    fi, bi = here()
    me = fi * 2 + bi
    slot = bi * NF + fi
    full_barrier()
    pltpu.make_async_copy(dop.at[slot], dop_r.at[me], recv_sems.at[0]).start()

    def body(d, _):
        t = lax.rem(slot + d, ND)
        pltpu.make_async_remote_copy(
            dop.at[t], dop_r.at[me], send_sems.at[0], recv_sems.at[0],
            device_id=(lax.rem(t, NF), t // NF), device_id_type=MESH,
        ).start()
        return 0

    lax.fori_loop(1, ND, body, 0)

    quarter = fi // 16
    place = lax.rem(fi, 16) * 2 + bi
    selfish = lax.rem(fi, 4) == quarter

    def body2(k, _):
        f, b = lax.rem(k, NG) * 4 + quarter, k // NG
        is_self = jnp.logical_and(f == fi, b == bi)

        @pl.when(is_self)
        def _():
            pltpu.make_async_copy(dsec.at[k], dsec_r.at[place], recv_sems.at[1]).start()

        @pl.when(jnp.logical_not(is_self))
        def _():
            pltpu.make_async_remote_copy(
                dsec.at[k], dsec_r.at[place], send_sems.at[1], recv_sems.at[1],
                device_id=(f, b), device_id_type=MESH,
            ).start()

        return 0

    lax.fori_loop(0, NB, body2, 0)

    def body3(d, _):
        is_self = d == me

        @pl.when(is_self)
        def _():
            pltpu.make_async_copy(wg.at[d - 48], wg_r.at[me], recv_sems.at[2]).start()

        @pl.when(jnp.logical_not(is_self))
        def _():
            pltpu.make_async_remote_copy(
                wg.at[d - 48], wg_r.at[me], send_sems.at[2], recv_sems.at[2],
                device_id=(d // 2, lax.rem(d, 2)), device_id_type=MESH,
            ).start()

        return 0

    lax.fori_loop(48, ND, body3, 0)

    wait_bytes(dop_r, recv_sems.at[0])
    wait_bytes(dop.at[pl.ds(0, ND - 1)], send_sems.at[0])
    wait_bytes(dsec_r, recv_sems.at[1])
    wait_bytes(dsec.at[pl.ds(0, NB - 1)], send_sems.at[1])

    @pl.when(jnp.logical_not(selfish))
    def _():
        wait_bytes(dsec.at[0], send_sems.at[1])

    wait_bytes(wg.at[pl.ds(0, 79)], send_sems.at[2])

    @pl.when(me >= 48)
    def _():
        wait_bytes(wg_r, recv_sems.at[2])

    @pl.when(me < 48)
    def _():
        wait_bytes(wg.at[0], send_sems.at[2])


def tail_kernel(gband, gq, out, gsum, quad, part, gq_r, send_sems, recv_sems):
    fi, bi = here()
    me = fi * 2 + bi
    full_barrier()
    mine = lax.rem(fi, 4)
    base = fi - mine
    pltpu.make_async_copy(gband.at[mine], quad.at[mine], recv_sems.at[0]).start()
    for d in range(1, 4):
        t = lax.rem(mine + d, 4)
        pltpu.make_async_remote_copy(
            gband.at[t], quad.at[mine], send_sems.at[0], recv_sems.at[0],
            device_id=(base + t, bi), device_id_type=MESH,
        ).start()

    def body(d, _):
        is_self = d == me

        @pl.when(is_self)
        def _():
            pltpu.make_async_copy(gq.at[d], gq_r.at[me], recv_sems.at[1]).start()

        @pl.when(jnp.logical_not(is_self))
        def _():
            pltpu.make_async_remote_copy(
                gq.at[d], gq_r.at[me], send_sems.at[1], recv_sems.at[1],
                device_id=(d // 2, lax.rem(d, 2)), device_id_type=MESH,
            ).start()

        return 0

    lax.fori_loop(0, 48, body, 0)

    wait_bytes(quad, recv_sems.at[0])
    part[...] = jnp.sum(quad[...].astype(F32), axis=0).astype(BF)
    pltpu.make_async_copy(part, out.at[fi], recv_sems.at[2]).start()

    def body2(d, _):
        pltpu.make_async_remote_copy(
            part, out.at[fi], send_sems.at[2], recv_sems.at[2],
            device_id=(lax.rem(fi + d, NF), bi), device_id_type=MESH,
        ).start()
        return 0

    lax.fori_loop(1, NF, body2, 0)

    @pl.when(me < 48)
    def _():
        wait_bytes(gq_r, recv_sems.at[1])
        x = gq_r[...].reshape(NG, 4, 2, 16, 128)
        gsum[...] = jnp.sum(x.astype(F32), axis=(0, 2))

    @pl.when(me >= 48)
    def _():
        gsum[...] = jnp.zeros_like(gsum)

    wait_bytes(out, recv_sems.at[2])
    wait_bytes(gband.at[pl.ds(0, 3)], send_sems.at[0])
    wait_bytes(gq.at[pl.ds(0, 47)], send_sems.at[1])

    @pl.when(me >= 48)
    def _():
        wait_bytes(gq.at[0], send_sems.at[1])

    wait_bytes(out.at[pl.ds(0, NF - 1)], send_sems.at[2])


VM = pl.BlockSpec(memory_space=pltpu.VMEM)
SM = pl.BlockSpec(memory_space=pltpu.SMEM)
ANY = pl.BlockSpec(memory_space=pl.ANY)


def struct(shape, dtype):
    return jax.ShapeDtypeStruct(shape, dtype)


def remote(kernel, outs, cid, n_sem, args, out_specs=None, in_specs=None, scratch=()):
    shape = (n_sem,) if n_sem else ()
    return pl.pallas_call(
        kernel,
        out_shape=outs,
        in_specs=in_specs or [ANY] * len(args),
        out_specs=out_specs or ([ANY] * len(outs) if isinstance(outs, list) else ANY),
        scratch_shapes=list(scratch) + [pltpu.SemaphoreType.DMA(shape), pltpu.SemaphoreType.DMA(shape)],
        compiler_params=pltpu.CompilerParams(
            collective_id=cid, has_side_effects=True, vmem_limit_bytes=VMEM_LIMIT
        ),
    )(*args)


def whole(shape):
    return pl.BlockSpec(shape, lambda c: (0,) * len(shape))


def shards(spectrum, band_widths, band_weight, qkv_time, out_time, qkv_band, out_band, cotangent):
    fi, bi = here()
    me = fi * 2 + bi
    swap = [(0, 1), (1, 0)]
    head = lax.rem(fi, 4)

    cot = cotangent[0]
    cot_own = lax.dynamic_slice_in_dim(cot, bi * HF, HF, 1)
    cot_oth = lax.ppermute(lax.dynamic_slice_in_dim(cot, (1 - bi) * HF, HF, 1), "bands", swap)

    feat_own, lat_own, lat_away = pl.pallas_call(
        prep_kernel,
        out_shape=[struct((NG, FB, W), BF), struct((NG, HF, D), BF), struct((NG, HF, D), BF)],
        in_specs=[SM, VM, VM],
        out_specs=[VM, VM, VM],
        compiler_params=pltpu.CompilerParams(vmem_limit_bytes=VMEM_LIMIT),
    )(band_widths, spectrum[0], band_weight)

    feat = remote(send_feat_kernel, struct((NF, FB, W), BF), 1, 0, (feat_own,)).reshape(T, W)
    lat_oth = lax.ppermute(lat_away, "bands", swap)

    wh = lax.dynamic_index_in_dim(qkv_time.reshape(D, 3, 4, 64), head, 2, keepdims=False).reshape(D, 192)
    cc, sc = rotary_tables(np.arange(NQ) * BQ)
    cr, sr = rotary_tables(np.arange(BQ))
    tables = tuple(jnp.asarray(x) for x in (cc, sc, cr, sr))
    table_specs = [whole((NQ, 128)), whole((NQ, 128)), whole((BQ, 128)), whole((BQ, 128))]
    params = pltpu.CompilerParams(
        dimension_semantics=("arbitrary",), vmem_limit_bytes=VMEM_LIMIT
    )

    e, q, k, v, ol, op = pl.pallas_call(
        fwd_kernel,
        grid=(NQ,),
        out_shape=[struct((T, T), BF), struct((T, 128), BF), struct((T, 128), BF), struct((T, 128), BF),
                   struct((T, 128), F32), struct((ND, 16, 128), BF)],
        in_specs=[whole((T, W)), whole((NG, W, D)), whole((D, 192))] + table_specs,
        out_specs=[pl.BlockSpec((BQ, T), lambda c: (c, 0)), whole((T, 128)), whole((T, 128)), whole((T, 128)),
                   pl.BlockSpec((BQ, 128), lambda c: (c, 0)), pl.BlockSpec((8, 16, 128), lambda c: (c, 0, 0))],
        scratch_shapes=[pltpu.VMEM((8, 128), F32)],
        compiler_params=params,
        cost_estimate=pl.CostEstimate(flops=2 * 2 * T * T * 256, bytes_accessed=2 * T * T, transcendentals=T * T),
    )(feat, band_weight, wh, *tables)

    att = remote(send_att_kernel, struct((ND, 16, 128), BF), 2, 0, (op,)).reshape(NB, 4, 16, 128)

    cb, sb = rotary_tables(np.arange(256) // 8)
    lat_keep, lat_send, dsec, dop, wg = pl.pallas_call(
        band_kernel,
        out_shape=[struct((NG, HF, D), BF), struct((NG, HF, D), BF), struct((NB, HF, D), BF),
                   struct((NB, 4, 16, 128), BF), struct((80, 16, D), BF)],
        in_specs=[VM] * 10,
        out_specs=[VM] * 5,
        scratch_shapes=[pltpu.VMEM((4, 256, D), F32), pltpu.VMEM((4, 256, D), F32), pltpu.VMEM((4, 256, 256), BF),
                        pltpu.VMEM((4, 256, 256), F32), pltpu.VMEM((256, D), F32), pltpu.VMEM((D, 768), F32),
                        pltpu.VMEM((256, D), F32)],
        compiler_params=pltpu.CompilerParams(vmem_limit_bytes=VMEM_LIMIT),
    )(lat_own, lat_oth, cot_own, cot_oth, att, out_time, qkv_band, out_band, jnp.asarray(cb), jnp.asarray(sb))

    lat_recv = lax.ppermute(lat_send, "bands", swap)
    dop_r, dsec_r, wg_r = remote(
        send_back_kernel,
        [struct((ND, 16, 128), BF), struct((NB, HF, D), BF), struct((ND, 16, D), BF)],
        3, 3, (dop.reshape(ND, 16, 128), dsec, wg),
    )

    gband, gq, wsum = pl.pallas_call(
        bwd_kernel,
        grid=(NQ,),
        out_shape=[struct((4, 32, D), BF), struct((48, 16, 128), BF), struct((16, D), F32)],
        in_specs=[pl.BlockSpec((BQ, T), lambda c: (c, 0)), whole((T, W)), whole((NG, W, D)), whole((D, 192))]
        + table_specs
        + [whole((T, 128)), whole((T, 128)), whole((T, 128)), pl.BlockSpec((BQ, 128), lambda c: (c, 0)),
           pl.BlockSpec((8, 16, 128), lambda c: (c, 0, 0)), whole((1024, D)), whole((ND, 16, D))],
        out_specs=[whole((4, 32, D)), whole((48, 16, 128)), whole((16, D))],
        scratch_shapes=[pltpu.VMEM((T, 128), F32), pltpu.VMEM((128, T), F32), pltpu.VMEM((W, D), F32),
                        pltpu.VMEM((D, 192), F32)],
        compiler_params=params,
        cost_estimate=pl.CostEstimate(flops=4 * 2 * T * T * 256, bytes_accessed=2 * T * T, transcendentals=0),
    )(e, feat, band_weight, wh, *tables, q, k, v, ol, dop_r, dsec_r.reshape(1024, D), wg_r)

    out, gsum = remote(
        tail_kernel,
        [struct((NF, 32, D), BF), struct((4, 16, 128), F32)],
        4, 3, (gband, gq),
        in_specs=[VM, VM],
        out_specs=[VM, VM],
        scratch=[pltpu.VMEM((4, 32, D), BF), pltpu.VMEM((32, D), BF), pltpu.VMEM((ND, 16, 128), BF)],
    )
    band_grad = out.reshape(NG, W, D).astype(F32)

    lat_lo = jnp.where(bi == 0, lat_keep, lat_recv)
    lat_hi = jnp.where(bi == 0, lat_recv, lat_keep)
    latent = jnp.concatenate([lat_lo, lat_hi], axis=1)[None]

    gt = jnp.stack([gsum[:, :8, :64], gsum[:, :8, 64:], gsum[:, 8:, :64]])
    share_t = gt.transpose(2, 0, 1, 3).reshape(-1)
    share_q = wsum.reshape(2, 8, D).transpose(1, 0, 2).reshape(-1)
    share = jnp.where(me < 48, share_t, jnp.where((me >= 64) & (me < 112), share_q, wsum.reshape(-1)))
    return (latent, band_grad, share)


def solution(mesh):
    placed = (
        P(None, "frames", None),
        P(),
        P("bands", None, None),
        P(),
        P(),
        P(),
        P(),
        P(None, "bands", "frames", None),
    )
    return jax.shard_map(
        shards,
        mesh=mesh,
        in_specs=placed,
        out_specs=(
            P(None, "bands", "frames", None),
            P("bands", None, None),
            P(("frames", "bands")),
        ),
        check_vma=False,
    )
```

```python
import math

import jax
import jax.numpy as jnp
import numpy as np
from jax import lax
from jax.experimental import pallas as pl
from jax.experimental.pallas import tpu as pltpu
from jax.sharding import PartitionSpec as P

EPS = 1e-05
THETA = 10000.0
NB = 32
NG = 16
NF = 64
ND = 128
FB = 64
HF = 32
T = 4096
D = 384
W = 128
BQ = 256
NQ = T // BQ
CF = 512
CB = 1024
LOG2E = math.log2(math.e)
BF = jnp.bfloat16
F32 = jnp.float32
MESH = pl.DeviceIdType.MESH
VMEM_LIMIT = 63 * 1024 * 1024

NN = (((1,), (0,)), ((), ()))
NT = (((1,), (1,)), ((), ()))
TN = (((0,), (0,)), ((), ()))


def mm(a, b, dims=NN):
    return lax.dot_general(a, b, dims, preferred_element_type=F32)


def lanes(shape):
    return lax.broadcasted_iota(jnp.int32, shape, len(shape) - 1)


def swap_halves(x):
    lane = lanes(x.shape)
    ax = len(x.shape) - 1
    return jnp.where(lane % 64 < 32, pltpu.roll(x, 96, ax), pltpu.roll(x, 32, ax))


def rotary_tables(positions):
    i = np.arange(128) % 32
    freq = np.exp(i.astype(np.float64) * (-2.0 * math.log(THETA) / 64))
    sign = np.where(np.arange(128) % 64 < 32, -1.0, 1.0)
    ang = np.asarray(positions, np.float64)[:, None] * freq[None, :]
    return np.cos(ang).astype(np.float32), (np.sin(ang) * sign).astype(np.float32)


def here():
    return lax.axis_index("frames"), lax.axis_index("bands")


def wait_bytes(ref, sem):
    pltpu.make_async_copy(ref, ref, sem).wait()


def copy_to(src, dst, send_sem, recv_sem, frames, bands):
    pltpu.make_async_remote_copy(
        src, dst, send_sem, recv_sem, device_id=(frames, bands), device_id_type=MESH
    ).start()


def copy_out(src, dst, send_sem, recv_sem, frames, bands):
    fi, bi = here()
    mine = jnp.logical_and(frames == fi, bands == bi)

    @pl.when(mine)
    def _():
        pltpu.make_async_copy(src, dst, recv_sem).start()

    @pl.when(jnp.logical_not(mine))
    def _():
        copy_to(src, dst, send_sem, recv_sem, frames, bands)


def loop(lo, hi, body):
    def step(i, carry):
        body(i)
        return carry

    lax.fori_loop(lo, hi, step, 0)


def rows_of(j, n=BQ):
    return pl.ds(pl.multiple_of(j * n, n), n)


def angles_at(c, cc, sc, cr, sr):
    ca = cc[pl.ds(c, 1), :]
    sa = sc[pl.ds(c, 1), :]
    return ca * cr[...] - sa * sr[...], sa * cr[...] + ca * sr[...]


def normed_rows(feat_rows, bwk):
    lat = mm(feat_rows, bwk).astype(BF).astype(F32)
    r = lax.rsqrt(jnp.mean(lat * lat, axis=-1, keepdims=True) + EPS)
    return lat * r, r


def own_columns(qt, wh):
    head = lax.rem(lax.axis_index("frames"), 4)
    parts = []
    for s in range(3):
        x = qt[:, pl.ds(pl.multiple_of(s * 256 + (head // 2) * 128, 128), 128)].astype(F32)
        parts.append(jnp.where(lax.rem(head, 2) == 1, pltpu.roll(x, 64, 1), x))
    low = lanes((D, 128)) < 64
    wh[:, 0:128] = jnp.where(low, parts[0], pltpu.roll(parts[1], 64, 1)).astype(BF)
    wh[:, 128:256] = jnp.where(low, parts[2], 0.0).astype(BF)


def make_features(widths, spec, bw, feat, lat):
    bi = lax.axis_index("bands")
    start = jnp.int32(0)
    for j in range(NG):
        start = start + jnp.where(bi == 1, widths[j], 0)

    def one(k, start):
        w = widths[bi * NG + k]
        col = lax.broadcasted_iota(jnp.int32, (spec.shape[1], W), 0)
        lane = lanes((spec.shape[1], W))
        pick = jnp.logical_and(col - lane == 2 * start, lane < 2 * w)
        y = mm(spec[...], jnp.where(pick, 1.0, 0.0).astype(BF)).astype(BF)
        feat[k] = y
        lat[k] = mm(y, bw[rows_of(k, W), 0:D]).astype(BF)
        return start + w

    lax.fori_loop(0, NG, one, start)


def project(feat, bwk, wh, tables, q_s, k_s, kt_s, v_s, vt_s):
    def pre(j):
        rows = rows_of(j)
        f = feat[pl.ds(pl.multiple_of(j * 4, 4), 4)].reshape(BQ, W)
        n, _r = normed_rows(f, bwk[...])
        proj = mm(n.astype(BF), wh[...])
        co, si = angles_at(j, *tables)
        a = proj[:, :128]
        a = a * co + swap_halves(a) * si
        low = lanes(a.shape) < 64
        q_s[rows, :] = (a * (0.125 * LOG2E)).astype(BF)
        k = jnp.where(low, pltpu.roll(a, 64, 1), 0.0)
        k_s[rows, :] = k.astype(BF)
        kt_s[:, rows] = k.T[:64].astype(BF)
        v = jnp.where(low, proj[:, 128:], 1.0)
        v_s[rows, :] = v.astype(BF)
        vt_s[:, rows] = v.T.astype(BF)

    loop(0, NQ, pre)


def attend(blk, q_s, kt_s, v_s, e_s, s_s, ol, op):
    rows = rows_of(blk)
    q = q_s[rows, :][:, :64]
    top = jnp.full((BQ, 128), -jnp.inf, F32)
    for j in range(T // CF):
        cols = slice(j * CF, (j + 1) * CF)
        s = mm(q, kt_s[:, cols])
        s_s[:, cols] = s
        for i in range(CF // 128):
            top = jnp.maximum(top, s[:, 128 * i:128 * i + 128])
    top = jnp.max(top, axis=1, keepdims=True)
    res = jnp.zeros((BQ, 128), F32)
    for j in range(T // CF):
        cols = slice(j * CF, (j + 1) * CF)
        e = jnp.exp2(s_s[:, cols] - top).astype(BF)
        e_s[rows, cols] = e
        res = res + mm(e, v_s[cols, :])
    rl = 1.0 / res
    low = lanes(res.shape) < 64
    o = res * pltpu.roll(rl, 64, 1)
    ol[rows, :] = jnp.where(low, o, rl)
    o4 = o.reshape(BQ // HF, 2, 16, 128)
    low3 = lanes((BQ // HF, 16, 128)) < 64
    op[pl.ds(pl.multiple_of(blk * 8, 8), 8)] = jnp.where(low3, o4[:, 0], pltpu.roll(o4[:, 1], 64, 2)).astype(BF)


def attend_back(c, e_s, q_s, k_s, vt_s, ol, dop, t_s):
    rows = rows_of(c)
    x = dop[pl.ds(pl.multiple_of(c * 8, 8), 8)].astype(F32)
    do = jnp.concatenate([x[:, None], pltpu.roll(x, 64, 2)[:, None]], axis=1).reshape(BQ, 128)
    o = ol[rows, :]
    lane = lanes((BQ, 128))
    do = jnp.where(lane < 64, do * pltpu.roll(o, 64, 1), 0.0)
    delta = jnp.sum(do * o, axis=1, keepdims=True)
    hi = delta.astype(BF).astype(F32)
    aug = jnp.where(lane == 64, -hi, jnp.where(lane == 65, hi - delta, do)).astype(BF)
    do_t = do.T[:64].astype(BF)
    q_t = q_s[rows, :].astype(F32).T[:64].astype(BF)
    dq = jnp.zeros((BQ, 128), F32)
    for j in range(T // CB):
        cols = slice(j * CB, (j + 1) * CB)
        e = e_s[rows, cols]
        ds = (e.astype(F32) * mm(aug, vt_s[:, cols])).astype(BF)
        dq = dq + mm(ds, k_s[cols, :])
        t_s[0:64, cols] += mm(do_t, e)
        t_s[64:128, cols] += mm(q_t, ds)
    ol[rows, :] = dq * 0.125


def project_back(feat, bwk, wh, tables, dq_s, t_s, gb_s, gq_s):
    low = lanes((BQ, 128)) < 64
    gq_s[...] = jnp.zeros_like(gq_s)

    def post(j):
        rows = rows_of(j)
        tx = t_s[0:128, rows].T
        a = jnp.where(low, dq_s[rows, :], tx * math.log(2.0)).astype(BF).astype(F32)
        co, si = angles_at(j, *tables)
        a = a * co - swap_halves(a) * si
        dproj = jnp.concatenate([a, jnp.where(low, tx, 0.0)], axis=1).astype(BF)
        dn = mm(dproj, wh[...], NT).astype(BF).astype(F32)
        f = feat[pl.ds(pl.multiple_of(j * 4, 4), 4)].reshape(BQ, W)
        n, r = normed_rows(f, bwk[...])
        dlat = (r * (dn - n * jnp.mean(n * dn, axis=1, keepdims=True))).astype(BF)
        gb_s[...] += mm(f, dlat, TN)
        gq_s[...] += mm(n.astype(BF), dproj, TN)

    loop(0, NQ, post)


def band_layer(lat_all, lat_oth, cot_own, cot_oth, att, w_ot, w_qb, w_ob, cb, sb,
               lat_keep, lat_send, dsec_out, dop_out, wg_out, s_s, att_s, g_ot, g_qb, g_ob):
    bi = lax.axis_index("bands")
    own = pl.ds(pl.multiple_of(bi * 128, 128), 128)
    oth = pl.ds(pl.multiple_of((1 - bi) * 128, 128), 128)
    mine = pl.ds(pl.multiple_of(bi * HF, HF), HF)

    def lat_at(g):
        return pl.ds(pl.multiple_of(g * D, 128), D)

    def cot_at(g):
        return pl.ds(pl.multiple_of(4 * D + g * D, 128), D)

    def do_at(g):
        return pl.ds(pl.multiple_of(8 * D + g * 256, 128), 256)

    for x, at, where in ((lat_all[:, mine, :], lat_at, own), (lat_oth[...], lat_at, oth),
                         (cot_own[...], cot_at, own), (cot_oth[...], cot_at, oth)):
        x = x.astype(F32)
        for g in range(4):
            s_s[where, at(g)] = x[:, 8 * g:8 * g + 8, :].reshape(128, D)
    low = lanes((256, 128)) < 64

    def pair(a, b, p):
        if p == 0:
            return jnp.where(low, a, pltpu.roll(b, 64, 1))
        return jnp.where(low, pltpu.roll(a, 64, 1), b)

    for j in range(2):
        x0 = att[:, 2 * j].astype(F32)
        x1 = att[:, 2 * j + 1].astype(F32)
        for g in range(4):
            p, rr = g // 2, g % 2
            a = x0[:, 8 * rr:8 * rr + 8, :].reshape(256, 128)
            b = x1[:, 8 * rr:8 * rr + 8, :].reshape(256, 128)
            att_s[g, :, 128 * j:128 * j + 128] = pair(a, b, p).astype(BF)

    g_ot[...] = jnp.zeros_like(g_ot)
    g_qb[...] = jnp.zeros_like(g_qb)
    g_ob[...] = jnp.zeros_like(g_ob)

    def group(g):
        att_g = att_s[g]
        cot = s_s[:, cot_at(g)]
        cot_b = cot.astype(BF)
        sec = (s_s[:, lat_at(g)] + mm(att_g, w_ot[...])).astype(BF).astype(F32)
        r = lax.rsqrt(jnp.mean(sec * sec, axis=-1, keepdims=True) + EPS)
        n = sec * r
        nb = n.astype(BF)
        proj = mm(nb, w_qb[...])
        dbatt = mm(cot_b, w_ob[...], NT)
        co, si = cb[...], sb[...]
        row_t = lax.broadcasted_iota(jnp.int32, (256, 256), 0) % 8
        col_t = lax.broadcasted_iota(jnp.int32, (256, 256), 1) % 8
        same = row_t == col_t
        batts, dqs, dks, dvs = [], [], [], []
        for j in range(2):
            q = proj[:, 128 * j:128 * j + 128]
            k = proj[:, 256 + 128 * j:384 + 128 * j]
            v = proj[:, 512 + 128 * j:640 + 128 * j].astype(BF)
            q = ((q * co + swap_halves(q) * si) * 0.125).astype(BF)
            k = (k * co + swap_halves(k) * si).astype(BF)
            do = dbatt[:, 128 * j:128 * j + 128].astype(BF)
            outs = []
            for hh in range(2):
                part = low if hh == 0 else jnp.logical_not(low)
                zero = jnp.zeros((), BF)
                qm = jnp.where(part, q, zero)
                dm = jnp.where(part, do, zero)
                s = jnp.where(same, mm(qm, k, NT), -jnp.inf)
                e = jnp.exp(s - jnp.max(s, axis=1, keepdims=True))
                p = e * (1.0 / jnp.sum(e, axis=1, keepdims=True))
                pb = p.astype(BF)
                pf = pb.astype(F32)
                o = mm(pb, v)
                dp = mm(dm, v, NT)
                ds = (pf * (dp - jnp.sum(pf * dp, axis=1, keepdims=True))).astype(BF)
                outs.append((o, mm(ds, k), mm(ds, q, TN), mm(pb, do, TN)))
            batts.append(jnp.where(low, outs[0][0], outs[1][0]).astype(BF))
            dq = (jnp.where(low, outs[0][1], outs[1][1]) * 0.125).astype(BF).astype(F32)
            dk = jnp.where(low, outs[0][2], outs[1][2]).astype(BF).astype(F32)
            dqs.append((dq * co - swap_halves(dq) * si).astype(BF))
            dks.append((dk * co - swap_halves(dk) * si).astype(BF))
            dvs.append(jnp.where(low, outs[0][3], outs[1][3]).astype(BF))
        batt = jnp.concatenate(batts, axis=1)
        dproj = jnp.concatenate(dqs + dks + dvs, axis=1)
        s_s[:, lat_at(g)] = sec + mm(batt, w_ob[...])
        dn = mm(dproj, w_qb[...], NT).astype(BF).astype(F32)
        dsec = (cot + r * (dn - n * jnp.mean(n * dn, axis=1, keepdims=True))).astype(BF)
        s_s[:, cot_at(g)] = dsec.astype(F32)
        s_s[:, do_at(g)] = mm(dsec, w_ot[...], NT)
        g_ob[...] += mm(batt, cot_b, TN)
        g_qb[...] += mm(nb, dproj, TN)
        g_ot[...] += mm(att_g, dsec, TN)

    loop(0, 4, group)

    for j in range(2):
        for hh in range(2):
            parts = []
            for rr in range(2):
                a = s_s[:, do_at(rr)][:, 128 * j:128 * j + 128]
                b = s_s[:, do_at(2 + rr)][:, 128 * j:128 * j + 128]
                parts.append(pair(a, b, hh).reshape(NB, 8, 128))
            dop_out[:, 2 * j + hh] = jnp.concatenate(parts, axis=1).astype(BF)

    def rest():
        dsec_out[...] = jnp.concatenate(
            [s_s[:, cot_at(g)].reshape(NB, 8, D) for g in range(4)], axis=1
        ).astype(BF)
        for ref, where in ((lat_keep, own), (lat_send, oth)):
            ref[...] = jnp.concatenate(
                [s_s[where, lat_at(g)].reshape(NG, 8, D) for g in range(4)], axis=1
            ).astype(BF)
        wg_out[0:16] = g_ot[...].reshape(16, 16, D).astype(BF)
        wg_out[16:64] = jnp.concatenate(
            [g_qb[:, :D].reshape(48, 8, D), g_qb[:, D:].reshape(48, 8, D)], axis=1
        ).astype(BF)
        wg_out[64:80] = g_ob[...].reshape(16, 16, D).astype(BF)

    return rest


def kernel(widths, spec, bw, qt, w_ot, w_qb, w_ob, cot, cc, sc, cr, sr, cb, sb,
           latent, out, wg_r, gsum, wsum,
           e_s, s_s, feat_own, feat, lat_all, lat_oth, cot_own, cot_oth, wh, q_s, k_s, kt_s, v_s, vt_s,
           ol, op, att, att_s, g_ot, g_qb, g_ob, lat_keep, lat_send, dsec, dop, wg, dop_r, dsec_r,
           bwk, gb_s, gq_s, gband, gq, quad, part, gq_r, send, recv, local):
    fi, bi = here()
    me = fi * 2 + bi
    slot = bi * NF + fi
    head = lax.rem(fi, 4)
    tables = (cc, sc, cr, sr)
    mine = pl.ds(pl.multiple_of(bi * HF, HF), HF)
    other = pl.ds(pl.multiple_of((1 - bi) * HF, HF), HF)

    bw_at = e_s.at[pl.ds(0, NG * W), pl.ds(0, D)]
    bw_copy = pltpu.make_async_copy(bw, bw_at, local.at[0])
    bw_copy.start()
    cot_copy = pltpu.make_async_copy(cot.at[:, mine, :], cot_own, local.at[1])
    cot_copy.start()

    barrier = pltpu.get_barrier_semaphore()

    def greet(d):
        t = lax.rem(me + d, ND)
        pl.semaphore_signal(barrier, inc=1, device_id=(t // 2, lax.rem(t, 2)), device_id_type=MESH)

    loop(1, ND, greet)

    own_columns(qt, wh)
    bw_copy.wait()
    make_features(widths, spec, e_s, feat_own, lat_all)
    bwk[...] = e_s[rows_of(fi // 4, W), 0:D]
    pl.semaphore_wait(barrier, ND - 1)

    pltpu.make_async_copy(feat_own.at[fi // 4], feat.at[fi], recv.at[0]).start()

    def give_features(d):
        t = lax.rem(fi + d, NF)
        copy_to(feat_own.at[t // 4], feat.at[fi], send.at[0], recv.at[0], t, bi)

    loop(1, NF, give_features)
    copy_to(lat_all.at[:, other, :], lat_oth, send.at[1], recv.at[1], fi, 1 - bi)
    copy_to(cot.at[:, other, :], cot_oth, send.at[2], recv.at[2], fi, 1 - bi)

    wait_bytes(feat, recv.at[0])
    project(feat, bwk, wh, tables, q_s, k_s, kt_s, v_s, vt_s)

    def forward(c):
        blk = lax.rem(c + fi // 4, NQ)
        attend(blk, q_s, kt_s, v_s, e_s, s_s, ol, op)

        def give(u):
            d = blk * 8 + u
            copy_out(op.at[d], att.at[slot], send.at[3], recv.at[3], d // 2, lax.rem(d, 2))

        loop(0, 8, give)

    loop(0, NQ, forward)

    wait_bytes(lat_oth, recv.at[1])
    wait_bytes(cot_oth, recv.at[2])
    cot_copy.wait()
    wait_bytes(att, recv.at[3])
    rest = band_layer(
        lat_all, lat_oth, cot_own, cot_oth, att.reshape(NB, 4, 16, 128), w_ot, w_qb, w_ob, cb, sb,
        lat_keep, lat_send, dsec, dop.reshape(NB, 4, 16, 128), wg, s_s, att_s, g_ot, g_qb, g_ob)

    pltpu.make_async_copy(dop.at[slot], dop_r.at[me], recv.at[4]).start()

    def give_back(d):
        t = lax.rem(slot + d, ND)
        copy_to(dop.at[t], dop_r.at[me], send.at[4], recv.at[4], lax.rem(t, NF), t // NF)

    loop(1, ND, give_back)
    rest()

    quarter = fi // 16
    place = lax.rem(fi, 16) * 2 + bi

    def give_second(k):
        copy_out(dsec.at[k], dsec_r.at[place], send.at[5], recv.at[5],
                 lax.rem(k, NG) * 4 + quarter, k // NG)

    loop(0, NB, give_second)
    copy_to(lat_send, latent.at[:, mine, :], send.at[7], recv.at[7], fi, 1 - bi)
    lat_copy = pltpu.make_async_copy(lat_keep, latent.at[:, mine, :], local.at[1])
    lat_copy.start()

    def give_weights(d):
        copy_out(wg.at[d - 48], wg_r.at[rows_of(me, 16)], send.at[6], recv.at[6], d // 2, lax.rem(d, 2))

    loop(48, ND, give_weights)

    s_s[0:128, :] = jnp.zeros((128, T), F32)
    wait_bytes(dop_r, recv.at[4])
    loop(0, NQ, lambda c: attend_back(c, e_s, q_s, k_s, vt_s, ol, dop_r, s_s))

    wait_bytes(dsec_r, recv.at[5])
    f = feat[pl.ds(pl.multiple_of(head * 16, 16), 16)].reshape(1024, W)
    gb_s[...] = mm(f, dsec_r[...].reshape(1024, D), TN)
    project_back(feat, bwk, wh, tables, ol, s_s, gb_s, gq_s)

    gband[...] = gb_s[...].reshape(4, 32, D).astype(BF)
    base = fi - head
    pltpu.make_async_copy(gband.at[head], quad.at[head], recv.at[8]).start()
    for d in range(1, 4):
        t = lax.rem(head + d, 4)
        copy_to(gband.at[t], quad.at[head], send.at[8], recv.at[8], base + t, bi)
    g = gq_s[...]
    gq[...] = jnp.concatenate(
        [g[:, :128].reshape(48, 8, 128), g[:, 128:].reshape(48, 8, 128)], axis=1
    ).astype(BF)
    loop(0, 48, lambda d: copy_out(gq.at[d], gq_r.at[me], send.at[9], recv.at[9], d // 2, lax.rem(d, 2)))

    wait_bytes(quad, recv.at[8])
    part[...] = jnp.sum(quad[...].astype(F32), axis=0).astype(BF)
    pltpu.make_async_copy(part, out.at[fi], recv.at[10]).start()

    def give_band(d):
        copy_to(part, out.at[fi], send.at[10], recv.at[10], lax.rem(fi + d, NF), bi)

    loop(1, NF, give_band)

    @pl.when(me < 48)
    def _():
        wsum[...] = jnp.zeros_like(wsum)
        wait_bytes(gq_r, recv.at[9])
        x = gq_r[...].reshape(NG, 4, 2, 16, 128)
        gsum[...] = jnp.sum(x.astype(F32), axis=(0, 2))

    @pl.when(me >= 48)
    def _():
        gsum[...] = jnp.zeros_like(gsum)
        wait_bytes(wg_r, recv.at[6])
        at = e_s.at[pl.ds(0, ND * 16), pl.ds(0, D)]
        fetch = pltpu.make_async_copy(wg_r, at, local.at[2])
        fetch.start()
        fetch.wait()
        wsum[...] = jnp.sum(e_s[0:ND * 16, 0:D].astype(F32).reshape(ND, 16, D), axis=0)

    wait_bytes(latent.at[:, other, :], recv.at[7])
    lat_copy.wait()
    wait_bytes(out, recv.at[10])
    wait_bytes(feat.at[pl.ds(0, NF - 1)], send.at[0])
    wait_bytes(lat_oth, send.at[1])
    wait_bytes(cot_oth, send.at[2])
    wait_bytes(op.at[pl.ds(0, ND - 1)], send.at[3])
    wait_bytes(dop.at[pl.ds(0, ND - 1)], send.at[4])
    wait_bytes(dsec.at[pl.ds(0, NB - 1)], send.at[5])
    wait_bytes(lat_send, send.at[7])
    wait_bytes(gband.at[pl.ds(0, 3)], send.at[8])
    wait_bytes(gq.at[pl.ds(0, 47)], send.at[9])
    wait_bytes(wg.at[pl.ds(0, 79)], send.at[6])
    wait_bytes(out.at[pl.ds(0, NF - 1)], send.at[10])

    @pl.when(head != quarter)
    def _():
        wait_bytes(dsec.at[0], send.at[5])

    @pl.when(me >= 48)
    def _():
        wait_bytes(gq.at[0], send.at[9])

    @pl.when(me < 48)
    def _():
        wait_bytes(wg.at[0], send.at[6])


VM = pl.BlockSpec(memory_space=pltpu.VMEM)
SM = pl.BlockSpec(memory_space=pltpu.SMEM)
ANY = pl.BlockSpec(memory_space=pl.ANY)


def struct(shape, dtype):
    return jax.ShapeDtypeStruct(shape, dtype)


def shards(spectrum, band_widths, band_weight, qkv_time, out_time, qkv_band, out_band, cotangent):
    fi, bi = here()
    me = fi * 2 + bi
    tables = rotary_tables(np.arange(NQ) * BQ) + rotary_tables(np.arange(BQ)) + rotary_tables(np.arange(256) // 8)
    tables = tuple(jnp.asarray(x) for x in tables)

    def vm(shape, dtype=BF):
        return pltpu.VMEM(shape, dtype)

    latent, out, _wg_r, gsum, wsum = pl.pallas_call(
        kernel,
        out_shape=[struct((NG, FB, D), BF), struct((NF, 32, D), BF), struct((ND * 16, D), BF),
                   struct((4, 16, 128), F32), struct((16, D), F32)],
        in_specs=[SM, VM, ANY, VM, VM, VM, VM, ANY] + [VM] * 6,
        out_specs=[ANY, ANY, ANY, VM, VM],
        scratch_shapes=[
            vm((T, T)), vm((BQ, T), F32), vm((NG, FB, W)), vm((NF, FB, W)), vm((NG, FB, D)),
            vm((NG, HF, D)), vm((NG, HF, D)), vm((NG, HF, D)), vm((D, 256)),
            vm((T, 128)), vm((T, 128)), vm((64, T)), vm((T, 128)), vm((128, T)),
            vm((T, 128), F32), vm((ND, 16, 128)), vm((ND, 16, 128)), vm((4, 256, 256)),
            vm((256, D), F32), vm((D, 768), F32), vm((256, D), F32),
            vm((NG, HF, D)), vm((NG, HF, D)), vm((NB, HF, D)), vm((ND, 16, 128)), vm((80, 16, D)),
            vm((ND, 16, 128)), vm((NB, HF, D)),
            vm((W, D)), vm((W, D), F32), vm((D, 256), F32), vm((4, 32, D)), vm((48, 16, 128)),
            vm((4, 32, D)), vm((32, D)), vm((ND, 16, 128)),
            pltpu.SemaphoreType.DMA((11,)), pltpu.SemaphoreType.DMA((11,)), pltpu.SemaphoreType.DMA((3,)),
        ],
        compiler_params=pltpu.CompilerParams(
            collective_id=1, has_side_effects=True, vmem_limit_bytes=VMEM_LIMIT
        ),
    )(band_widths, spectrum[0], band_weight.reshape(NG * W, D), qkv_time, out_time, qkv_band, out_band,
      cotangent[0], *tables)

    band_grad = out.reshape(NG, W, D).astype(F32)
    gt = jnp.stack([gsum[:, :8, :64], gsum[:, :8, 64:], gsum[:, 8:, :64]])
    share_t = gt.transpose(2, 0, 1, 3).reshape(-1)
    share_q = wsum.reshape(2, 8, D).transpose(1, 0, 2).reshape(-1)
    share = jnp.where(me < 48, share_t, jnp.where((me >= 64) & (me < 112), share_q, wsum.reshape(-1)))
    return (latent[None], band_grad, share)


def solution(mesh):
    placed = (
        P(None, "frames", None),
        P(),
        P("bands", None, None),
        P(),
        P(),
        P(),
        P(),
        P(None, "bands", "frames", None),
    )
    return jax.shard_map(
        shards,
        mesh=mesh,
        in_specs=placed,
        out_specs=(
            P(None, "bands", "frames", None),
            P("bands", None, None),
            P(("frames", "bands")),
        ),
        check_vma=False,
    )
```

```python
import math

import jax
import jax.numpy as jnp
import numpy as np
from jax import lax
from jax.experimental import pallas as pl
from jax.experimental.pallas import tpu as pltpu
from jax.sharding import PartitionSpec as P

EPS = 1e-05
THETA = 10000.0
NB = 32
NG = 16
NF = 64
ND = 128
FB = 64
HF = 32
T = 4096
D = 384
W = 128
BQ = 256
NQ = T // BQ
BP = 512
NP = T // BP
CF = 512
CB = 1024
LOG2E = math.log2(math.e)
BF = jnp.bfloat16
F32 = jnp.float32
MESH = pl.DeviceIdType.MESH
VMEM_LIMIT = 63 * 1024 * 1024

NN = (((1,), (0,)), ((), ()))
NT = (((1,), (1,)), ((), ()))
TN = (((0,), (0,)), ((), ()))


def mm(a, b, dims=NN):
    return lax.dot_general(a, b, dims, preferred_element_type=F32)


def lanes(shape):
    return lax.broadcasted_iota(jnp.int32, shape, len(shape) - 1)


def swap_halves(x):
    lane = lanes(x.shape)
    ax = len(x.shape) - 1
    return jnp.where(lane % 64 < 32, pltpu.roll(x, 96, ax), pltpu.roll(x, 32, ax))


def rotary_tables(positions):
    i = np.arange(128) % 32
    freq = np.exp(i.astype(np.float64) * (-2.0 * math.log(THETA) / 64))
    sign = np.where(np.arange(128) % 64 < 32, -1.0, 1.0)
    ang = np.asarray(positions, np.float64)[:, None] * freq[None, :]
    return np.cos(ang).astype(np.float32), (np.sin(ang) * sign).astype(np.float32)


def here():
    return lax.axis_index("frames"), lax.axis_index("bands")


def wait_bytes(ref, sem):
    pltpu.make_async_copy(ref, ref, sem).wait()


def copy_to(src, dst, send_sem, recv_sem, frames, bands):
    pltpu.make_async_remote_copy(
        src, dst, send_sem, recv_sem, device_id=(frames, bands), device_id_type=MESH
    ).start()


def copy_out(src, dst, send_sem, recv_sem, frames, bands):
    fi, bi = here()
    mine = jnp.logical_and(frames == fi, bands == bi)

    @pl.when(mine)
    def _():
        pltpu.make_async_copy(src, dst, recv_sem).start()

    @pl.when(jnp.logical_not(mine))
    def _():
        copy_to(src, dst, send_sem, recv_sem, frames, bands)


def loop(lo, hi, body):
    def step(i, carry):
        body(i)
        return carry

    lax.fori_loop(lo, hi, step, 0)


def rows_of(j, n=BQ):
    return pl.ds(pl.multiple_of(j * n, n), n)


def angles_at(c, cc, sc, cr, sr):
    ca = cc[pl.ds(c, 1), :]
    sa = sc[pl.ds(c, 1), :]
    return ca * cr[...] - sa * sr[...], sa * cr[...] + ca * sr[...]


def normed_rows(feat_rows, bwk):
    lat = mm(feat_rows, bwk).astype(BF).astype(F32)
    r = lax.rsqrt(jnp.mean(lat * lat, axis=-1, keepdims=True) + EPS)
    return lat * r, r


def own_columns(qt, wh):
    head = lax.rem(lax.axis_index("frames"), 4)
    parts = []
    for s in range(3):
        x = qt[:, pl.ds(pl.multiple_of(s * 256 + (head // 2) * 128, 128), 128)].astype(F32)
        parts.append(jnp.where(lax.rem(head, 2) == 1, pltpu.roll(x, 64, 1), x))
    low = lanes((D, 128)) < 64
    wh[:, 0:128] = jnp.where(low, parts[0], pltpu.roll(parts[1], 64, 1)).astype(BF)
    wh[:, 128:256] = jnp.where(low, parts[2], 0.0).astype(BF)


def make_features(widths, spec, bw, feat, lat):
    bi = lax.axis_index("bands")
    start = jnp.int32(0)
    for j in range(NG):
        start = start + jnp.where(bi == 1, widths[j], 0)

    def one(k, start):
        w = widths[bi * NG + k]
        col = lax.broadcasted_iota(jnp.int32, (spec.shape[1], W), 0)
        lane = lanes((spec.shape[1], W))
        pick = jnp.logical_and(col - lane == 2 * start, lane < 2 * w)
        y = mm(spec[...], jnp.where(pick, 1.0, 0.0).astype(BF)).astype(BF)
        feat[k] = y
        lat[k] = mm(y, bw[rows_of(k, W), 0:D]).astype(BF)
        return start + w

    lax.fori_loop(0, NG, one, start)


def project(feat, arrived, bwk, wh, tables, q_s, k_s, kt_s, v_s, vt_s):
    fi, _ = here()

    def pre(i):
        j = lax.rem(fi // 8 + 2 * NP - 1 - i, NP)
        rows = rows_of(j, BP)
        wait_bytes(feat.at[rows_of(j, 8)], arrived.at[j])
        f = feat[rows_of(j, 8)].reshape(BP, W)
        n, _r = normed_rows(f, bwk[...])
        proj = mm(n.astype(BF), wh[...])
        co, si = angles_at(j, *tables)
        a = proj[:, :128]
        a = a * co + swap_halves(a) * si
        low = lanes(a.shape) < 64
        q_s[rows, :] = (a * (0.125 * LOG2E)).astype(BF)
        k = jnp.where(low, pltpu.roll(a, 64, 1), 0.0)
        k_s[rows, :] = k.astype(BF)
        kt_s[:, rows] = k.T[:64].astype(BF)
        v = jnp.where(low, proj[:, 128:], 1.0)
        v_s[rows, :] = v.astype(BF)
        vt_s[:, rows] = v.T.astype(BF)

    loop(0, NP, pre)


def attend(blk, q_s, kt_s, v_s, e_s, s_s, ol, op):
    rows = rows_of(blk)
    q = q_s[rows, :][:, :64]
    top = jnp.full((BQ, 128), -jnp.inf, F32)
    for j in range(T // CF):
        cols = slice(j * CF, (j + 1) * CF)
        s = mm(q, kt_s[:, cols])
        s_s[:, cols] = s
        for i in range(CF // 128):
            top = jnp.maximum(top, s[:, 128 * i:128 * i + 128])
    top = jnp.max(top, axis=1, keepdims=True)
    res = jnp.zeros((BQ, 128), F32)
    for j in range(T // CF):
        cols = slice(j * CF, (j + 1) * CF)
        e = jnp.exp2(s_s[:, cols] - top).astype(BF)
        e_s[rows, cols] = e
        res = res + mm(e, v_s[cols, :])
    rl = 1.0 / res
    low = lanes(res.shape) < 64
    o = res * pltpu.roll(rl, 64, 1)
    ol[rows, :] = jnp.where(low, o, rl)
    o4 = o.reshape(BQ // HF, 2, 16, 128)
    low3 = lanes((BQ // HF, 16, 128)) < 64
    op[pl.ds(pl.multiple_of(blk * 8, 8), 8)] = jnp.where(low3, o4[:, 0], pltpu.roll(o4[:, 1], 64, 2)).astype(BF)


def attend_back(c, e_s, q_s, k_s, vt_s, ol, dop, t_s):
    rows = rows_of(c)
    x = dop[pl.ds(pl.multiple_of(c * 8, 8), 8)].astype(F32)
    do = jnp.concatenate([x[:, None], pltpu.roll(x, 64, 2)[:, None]], axis=1).reshape(BQ, 128)
    o = ol[rows, :]
    lane = lanes((BQ, 128))
    do = jnp.where(lane < 64, do * pltpu.roll(o, 64, 1), 0.0)
    delta = jnp.sum(do * o, axis=1, keepdims=True)
    hi = delta.astype(BF).astype(F32)
    aug = jnp.where(lane == 64, -hi, jnp.where(lane == 65, hi - delta, do)).astype(BF)
    do_t = do.T[:64].astype(BF)
    q_t = q_s[rows, :].astype(F32).T[:64].astype(BF)
    dq = jnp.zeros((BQ, 128), F32)
    for j in range(T // CB):
        cols = slice(j * CB, (j + 1) * CB)
        e = e_s[rows, cols]
        ds = (e.astype(F32) * mm(aug, vt_s[:, cols])).astype(BF)
        dq = dq + mm(ds, k_s[cols, :])
        t_s[0:64, cols] += mm(do_t, e)
        t_s[64:128, cols] += mm(q_t, ds)
    ol[rows, :] = dq * 0.125


def project_back(feat, bwk, wh, tables, dq_s, t_s, gb_s, dproj_s, n_s):
    low = lanes((BP, 128)) < 64

    def post(j):
        rows = rows_of(j, BP)
        tx = t_s[0:128, rows].T
        a = jnp.where(low, dq_s[rows, :], tx * math.log(2.0)).astype(BF).astype(F32)
        co, si = angles_at(j, *tables)
        a = a * co - swap_halves(a) * si
        dproj = jnp.concatenate([a, jnp.where(low, tx, 0.0)], axis=1).astype(BF)
        dn = mm(dproj, wh[...], NT).astype(BF).astype(F32)
        f = feat[rows_of(j, 8)].reshape(BP, W)
        n, r = normed_rows(f, bwk[...])
        dlat = (r * (dn - n * jnp.mean(n * dn, axis=1, keepdims=True))).astype(BF)
        gb_s[...] += mm(f, dlat, TN)
        dproj_s[rows, :] = dproj
        n_s[rows, :] = n.astype(BF)

    loop(0, NP, post)


def band_layer(lat_all, lat_oth, cot_own, cot_oth, att, w_ot, w_qb, w_ob, cb, sb,
               lat_keep, lat_send, dsec_out, dop_out, wg_out, s_s, att_s, g_ot, g_qb, g_ob, wait_att):
    bi = lax.axis_index("bands")
    own = pl.ds(pl.multiple_of(bi * 128, 128), 128)
    oth = pl.ds(pl.multiple_of((1 - bi) * 128, 128), 128)
    mine = pl.ds(pl.multiple_of(bi * HF, HF), HF)

    def lat_at(g):
        return pl.ds(pl.multiple_of(g * D, 128), D)

    def cot_at(g):
        return pl.ds(pl.multiple_of(4 * D + g * D, 128), D)

    def do_at(g):
        return pl.ds(pl.multiple_of(8 * D + g * 256, 128), 256)

    for x, at, where in ((lat_all[:, mine, :], lat_at, own), (lat_oth[...], lat_at, oth),
                         (cot_own[...], cot_at, own), (cot_oth[...], cot_at, oth)):
        x = x.astype(F32)
        for g in range(4):
            s_s[where, at(g)] = x[:, 8 * g:8 * g + 8, :].reshape(128, D)
    g_ot[...] = jnp.zeros_like(g_ot)
    g_qb[...] = jnp.zeros_like(g_qb)
    g_ob[...] = jnp.zeros_like(g_ob)
    low = lanes((256, 128)) < 64
    wait_att()

    def pair(a, b, p):
        if p == 0:
            return jnp.where(low, a, pltpu.roll(b, 64, 1))
        return jnp.where(low, pltpu.roll(a, 64, 1), b)

    for j in range(2):
        x0 = att[:, 2 * j].astype(F32)
        x1 = att[:, 2 * j + 1].astype(F32)
        for g in range(4):
            p, rr = g // 2, g % 2
            a = x0[:, 8 * rr:8 * rr + 8, :].reshape(256, 128)
            b = x1[:, 8 * rr:8 * rr + 8, :].reshape(256, 128)
            att_s[g, :, 128 * j:128 * j + 128] = pair(a, b, p).astype(BF)

    def group(g):
        att_g = att_s[g]
        cot = s_s[:, cot_at(g)]
        cot_b = cot.astype(BF)
        sec = (s_s[:, lat_at(g)] + mm(att_g, w_ot[...])).astype(BF).astype(F32)
        r = lax.rsqrt(jnp.mean(sec * sec, axis=-1, keepdims=True) + EPS)
        n = sec * r
        nb = n.astype(BF)
        proj = mm(nb, w_qb[...])
        dbatt = mm(cot_b, w_ob[...], NT)
        co, si = cb[...], sb[...]
        row_t = lax.broadcasted_iota(jnp.int32, (256, 256), 0) % 8
        col_t = lax.broadcasted_iota(jnp.int32, (256, 256), 1) % 8
        same = row_t == col_t
        batts, dqs, dks, dvs = [], [], [], []
        for j in range(2):
            q = proj[:, 128 * j:128 * j + 128]
            k = proj[:, 256 + 128 * j:384 + 128 * j]
            v = proj[:, 512 + 128 * j:640 + 128 * j].astype(BF)
            q = ((q * co + swap_halves(q) * si) * 0.125).astype(BF)
            k = (k * co + swap_halves(k) * si).astype(BF)
            do = dbatt[:, 128 * j:128 * j + 128].astype(BF)
            outs = []
            for hh in range(2):
                part = low if hh == 0 else jnp.logical_not(low)
                zero = jnp.zeros((), BF)
                qm = jnp.where(part, q, zero)
                dm = jnp.where(part, do, zero)
                s = jnp.where(same, mm(qm, k, NT), -jnp.inf)
                e = jnp.exp(s - jnp.max(s, axis=1, keepdims=True))
                p = e * (1.0 / jnp.sum(e, axis=1, keepdims=True))
                pb = p.astype(BF)
                pf = pb.astype(F32)
                o = mm(pb, v)
                dp = mm(dm, v, NT)
                ds = (pf * (dp - jnp.sum(pf * dp, axis=1, keepdims=True))).astype(BF)
                outs.append((o, mm(ds, k), mm(ds, q, TN), mm(pb, do, TN)))
            batts.append(jnp.where(low, outs[0][0], outs[1][0]).astype(BF))
            dq = (jnp.where(low, outs[0][1], outs[1][1]) * 0.125).astype(BF).astype(F32)
            dk = jnp.where(low, outs[0][2], outs[1][2]).astype(BF).astype(F32)
            dqs.append((dq * co - swap_halves(dq) * si).astype(BF))
            dks.append((dk * co - swap_halves(dk) * si).astype(BF))
            dvs.append(jnp.where(low, outs[0][3], outs[1][3]).astype(BF))
        batt = jnp.concatenate(batts, axis=1)
        dproj = jnp.concatenate(dqs + dks + dvs, axis=1)
        s_s[:, lat_at(g)] = sec + mm(batt, w_ob[...])
        dn = mm(dproj, w_qb[...], NT).astype(BF).astype(F32)
        dsec = (cot + r * (dn - n * jnp.mean(n * dn, axis=1, keepdims=True))).astype(BF)
        s_s[:, cot_at(g)] = dsec.astype(F32)
        s_s[:, do_at(g)] = mm(dsec, w_ot[...], NT)
        g_ob[...] += mm(batt, cot_b, TN)
        g_qb[...] += mm(nb, dproj, TN)
        g_ot[...] += mm(att_g, dsec, TN)

    loop(0, 4, group)

    for j in range(2):
        for hh in range(2):
            parts = []
            for rr in range(2):
                a = s_s[:, do_at(rr)][:, 128 * j:128 * j + 128]
                b = s_s[:, do_at(2 + rr)][:, 128 * j:128 * j + 128]
                parts.append(pair(a, b, hh).reshape(NB, 8, 128))
            dop_out[:, 2 * j + hh] = jnp.concatenate(parts, axis=1).astype(BF)

    def rest():
        dsec_out[...] = jnp.concatenate(
            [s_s[:, cot_at(g)].reshape(NB, 8, D) for g in range(4)], axis=1
        ).astype(BF)
        for ref, where in ((lat_keep, own), (lat_send, oth)):
            ref[...] = jnp.concatenate(
                [s_s[where, lat_at(g)].reshape(NG, 8, D) for g in range(4)], axis=1
            ).astype(BF)
        wg_out[0:16] = g_ot[...].reshape(16, 16, D).astype(BF)
        wg_out[16:64] = jnp.concatenate(
            [g_qb[:, :D].reshape(48, 8, D), g_qb[:, D:].reshape(48, 8, D)], axis=1
        ).astype(BF)
        wg_out[64:80] = g_ob[...].reshape(16, 16, D).astype(BF)

    return rest


def kernel(widths, spec_h, bw, qt_h, w_ot_h, w_qb_h, w_ob_h, cot, cc_h, sc_h, cr_h, sr_h, cb_h, sb_h,
           latent, out, wg_r, share,
           spec, qt, w_ot, w_qb, w_ob, cc, sc, cr, sr, cb, sb,
           e_s, s_s, feat_own, feat, lat_all, lat_oth, cot_own, cot_oth, wh, q_s, k_s, kt_s, v_s, vt_s,
           ol, op, att, att_s, g_ot, g_qb, g_ob, lat_keep, lat_send, dsec, dop, wg, dop_r, dsec_r,
           bwk, gb_s, gq_s, gband, gq, quad, part, gq_r, send, recv, local,
           feat_in, dop_in, out_in, staged):
    fi, bi = here()
    me = fi * 2 + bi
    slot = bi * NF + fi
    head = lax.rem(fi, 4)
    tables = (cc, sc, cr, sr)
    mine = pl.ds(pl.multiple_of(bi * HF, HF), HF)
    other = pl.ds(pl.multiple_of((1 - bi) * HF, HF), HF)

    barrier = pltpu.get_barrier_semaphore()

    def greet(d):
        t = lax.rem(me + d, ND)
        pl.semaphore_signal(barrier, inc=1, device_id=(t // 2, lax.rem(t, 2)), device_id_type=MESH)

    loop(1, ND, greet)

    bw_at = e_s.at[pl.ds(0, NG * W), pl.ds(0, D)]
    first = ((bw, bw_at), (spec_h, spec), (qt_h, qt))
    later = ((cc_h, cc), (sc_h, sc), (cr_h, cr), (sr_h, sr), (w_ot_h, w_ot), (w_qb_h, w_qb), (w_ob_h, w_ob),
             (cb_h, cb), (sb_h, sb), (cot.at[:, mine, :], cot_own))
    copies = [pltpu.make_async_copy(x, y, staged.at[i]) for i, (x, y) in enumerate(first + later)]
    for c in copies:
        c.start()
    for c in copies[:len(first)]:
        c.wait()
    own_columns(qt, wh)
    make_features(widths, spec, e_s, feat_own, lat_all)
    bwk[...] = e_s[rows_of(fi // 4, W), 0:D]
    for c in copies[len(first):]:
        c.wait()
    pl.semaphore_wait(barrier, ND - 1)

    pltpu.make_async_copy(feat_own.at[fi // 4], feat.at[fi], feat_in.at[fi // 8]).start()

    def give_features(d):
        t = lax.rem(fi + d, NF)
        copy_to(feat_own.at[t // 4], feat.at[fi], send.at[0], feat_in.at[fi // 8], t, bi)

    loop(1, NF, give_features)
    copy_to(lat_all.at[:, other, :], lat_oth, send.at[1], recv.at[1], fi, 1 - bi)
    copy_to(cot.at[:, other, :], cot_oth, send.at[2], recv.at[2], fi, 1 - bi)

    project(feat, feat_in, bwk, wh, tables, q_s, k_s, kt_s, v_s, vt_s)

    def forward(c):
        blk = lax.rem(c + fi // 4, NQ)
        attend(blk, q_s, kt_s, v_s, e_s, s_s, ol, op)

        def give(u):
            d = blk * 8 + u
            copy_out(op.at[d], att.at[slot], send.at[3], recv.at[3], d // 2, lax.rem(d, 2))

        loop(0, 8, give)

    loop(0, NQ, forward)

    wait_bytes(lat_oth, recv.at[1])
    wait_bytes(cot_oth, recv.at[2])
    rest = band_layer(
        lat_all, lat_oth, cot_own, cot_oth, att.reshape(NB, 4, 16, 128), w_ot, w_qb, w_ob, cb, sb,
        lat_keep, lat_send, dsec, dop.reshape(NB, 4, 16, 128), wg, s_s, att_s, g_ot, g_qb, g_ob,
        lambda: wait_bytes(att, recv.at[3]))

    group = fi // 4
    pltpu.make_async_copy(dop.at[slot], dop_r.at[me], dop_in.at[group]).start()
    copy_to(dop.at[(1 - bi) * NF + fi], dop_r.at[me], send.at[4], dop_in.at[group], fi, 1 - bi)

    def give_back(d):
        f = lax.rem(fi + d, NF)
        copy_to(dop.at[f], dop_r.at[me], send.at[4], dop_in.at[group], f, 0)
        copy_to(dop.at[NF + f], dop_r.at[me], send.at[4], dop_in.at[group], f, 1)

    loop(1, NF, give_back)
    rest()

    quarter = fi // 16
    place = lax.rem(fi, 16) * 2 + bi

    def give_second(k):
        copy_out(dsec.at[k], dsec_r.at[place], send.at[5], recv.at[5],
                 lax.rem(k, NG) * 4 + quarter, k // NG)

    loop(0, NB, give_second)
    copy_to(lat_send, latent.at[:, mine, :], send.at[7], recv.at[7], fi, 1 - bi)
    lat_copy = pltpu.make_async_copy(lat_keep, latent.at[:, mine, :], local.at[1])
    lat_copy.start()

    def give_weights(d):
        copy_out(wg.at[d - 48], wg_r.at[rows_of(me, 16)], send.at[6], recv.at[6], d // 2, lax.rem(d, 2))

    loop(48, ND, give_weights)

    s_s[0:128, :] = jnp.zeros((128, T), F32)

    def backward(i):
        c = lax.rem(group + 2 * NQ - 1 - i, NQ)
        wait_bytes(dop_r.at[rows_of(c, 8)], dop_in.at[c])
        attend_back(c, e_s, q_s, k_s, vt_s, ol, dop_r, s_s)

    loop(0, NQ, backward)

    wait_bytes(dsec_r, recv.at[5])
    f = feat[rows_of(head, 16)].reshape(1024, W)
    gb_s[...] = mm(f, dsec_r[...].reshape(1024, D), TN)
    dproj_s = e_s.at[:, pl.ds(0, 256)]
    n_s = e_s.at[:, pl.ds(256, D)]
    project_back(feat, bwk, wh, tables, ol, s_s, gb_s, dproj_s, n_s)

    gband[...] = gb_s[...].reshape(4, 32, D).astype(BF)
    base = fi - head
    pltpu.make_async_copy(gband.at[head], quad.at[head], recv.at[8]).start()
    for d in range(1, 4):
        t = lax.rem(head + d, 4)
        copy_to(gband.at[t], quad.at[head], send.at[8], recv.at[8], base + t, bi)

    gq_s[...] = jnp.zeros_like(gq_s)

    def weight(j):
        rows = rows_of(j, 1024)
        gq_s[...] += mm(n_s[rows, :], dproj_s[rows, :], TN)

    loop(0, 4, weight)

    chip, core = fi // 2, lax.rem(fi, 2)
    mate = fi + 1 - 2 * core
    wait_bytes(quad, recv.at[8])
    part[...] = jnp.sum(quad[...].astype(F32), axis=0).astype(BF)
    pltpu.make_async_copy(part, out.at[chip, core], out_in.at[chip // 4]).start()

    def give_band(d):
        copy_to(part, out.at[chip, core], send.at[10], out_in.at[chip // 4],
                lax.rem(chip + d, 32) * 2 + core, bi)

    loop(1, 32, give_band)

    g = gq_s[...]
    gq[...] = jnp.concatenate(
        [g[:, :128].reshape(48, 8, 128), g[:, 128:].reshape(48, 8, 128)], axis=1
    ).astype(BF)
    loop(0, 48, lambda d: copy_out(gq.at[d], gq_r.at[me], send.at[9], recv.at[9], d // 2, lax.rem(d, 2)))

    def pass_on(i):
        j = lax.rem(chip // 4 + 15 - i, 8)
        block = out.at[rows_of(j, 4), core]
        wait_bytes(block, out_in.at[j])
        copy_to(block, block, send.at[0], recv.at[10], mate, bi)

    low8 = lanes((8, 128)) < 64

    wait_bytes(feat.at[pl.ds(0, NF - 1)], send.at[0])
    loop(0, 8, pass_on)

    @pl.when(me < 48)
    def _():
        wait_bytes(gq_r, recv.at[9])
        x = jnp.sum(gq_r[...].reshape(NG, 4, 2, 16, 128).astype(F32), axis=(0, 2))
        for j in range(2):
            a, b = x[2 * j], x[2 * j + 1]
            share[pl.ds(j, 8, stride=6), :] = jnp.where(low8, a[:8], pltpu.roll(b[:8], 64, 1))
            share[pl.ds(2 + j, 8, stride=6), :] = jnp.where(low8, pltpu.roll(a[:8], 64, 1), b[:8])
            share[pl.ds(4 + j, 8, stride=6), :] = jnp.where(low8, a[8:], pltpu.roll(b[8:], 64, 1))

    @pl.when(me >= 48)
    def _():
        wait_bytes(wg_r, recv.at[6])
        at = e_s.at[pl.ds(0, ND * 16), pl.ds(1024, D)]
        fetch = pltpu.make_async_copy(wg_r, at, local.at[2])
        fetch.start()
        fetch.wait()
        x = jnp.sum(e_s[0:ND * 16, 1024:1024 + D].astype(F32).reshape(ND, 16, D), axis=0)
        wide = jnp.logical_and(me >= 64, me < 112)

        @pl.when(wide)
        def _():
            for j in range(3):
                share[pl.ds(j, 8, stride=6), :] = x[:8, 128 * j:128 * j + 128]
                share[pl.ds(3 + j, 8, stride=6), :] = x[8:, 128 * j:128 * j + 128]

        @pl.when(jnp.logical_not(wide))
        def _():
            for j in range(3):
                share[pl.ds(j, 16, stride=3), :] = x[:, 128 * j:128 * j + 128]

    wait_bytes(latent.at[:, other, :], recv.at[7])
    lat_copy.wait()
    wait_bytes(out.at[:, 1 - core], recv.at[10])
    wait_bytes(out.at[:, core], send.at[0])
    wait_bytes(lat_oth, send.at[1])
    wait_bytes(cot_oth, send.at[2])
    wait_bytes(op.at[pl.ds(0, ND - 1)], send.at[3])
    wait_bytes(dop.at[pl.ds(0, ND - 1)], send.at[4])
    wait_bytes(dsec.at[pl.ds(0, NB - 1)], send.at[5])
    wait_bytes(lat_send, send.at[7])
    wait_bytes(gband.at[pl.ds(0, 3)], send.at[8])
    wait_bytes(gq.at[pl.ds(0, 47)], send.at[9])
    wait_bytes(wg.at[pl.ds(0, 79)], send.at[6])
    wait_bytes(out.at[pl.ds(0, 31), core], send.at[10])

    @pl.when(head != quarter)
    def _():
        wait_bytes(dsec.at[0], send.at[5])

    @pl.when(me >= 48)
    def _():
        wait_bytes(gq.at[0], send.at[9])

    @pl.when(me < 48)
    def _():
        wait_bytes(wg.at[0], send.at[6])


VM = pl.BlockSpec(memory_space=pltpu.VMEM)
SM = pl.BlockSpec(memory_space=pltpu.SMEM)
ANY = pl.BlockSpec(memory_space=pl.ANY)


def struct(shape, dtype):
    return jax.ShapeDtypeStruct(shape, dtype)


def shards(spectrum, band_widths, band_weight, qkv_time, out_time, qkv_band, out_band, cotangent):
    tables = rotary_tables(np.arange(NP) * BP) + rotary_tables(np.arange(BP)) + rotary_tables(np.arange(256) // 8)
    tables = tuple(jnp.asarray(x) for x in tables)

    def vm(shape, dtype=BF):
        return pltpu.VMEM(shape, dtype)

    latent, out, _wg_r, share = pl.pallas_call(
        kernel,
        out_shape=[struct((NG, FB, D), BF), struct((32, 2, 32, D), BF), struct((ND * 16, D), BF),
                   struct((48, 128), F32)],
        in_specs=[SM] + [ANY] * 13,
        out_specs=[ANY, ANY, ANY, VM],
        scratch_shapes=[
            vm((FB, 1280)), vm((D, 768)), vm((256, D)), vm((D, 768)), vm((256, D)),
            vm((NP, 128), F32), vm((NP, 128), F32), vm((BP, 128), F32), vm((BP, 128), F32),
            vm((256, 128), F32), vm((256, 128), F32),
            vm((T, T)), vm((BQ, T), F32), vm((NG, FB, W)), vm((NF, FB, W)), vm((NG, FB, D)),
            vm((NG, HF, D)), vm((NG, HF, D)), vm((NG, HF, D)), vm((D, 256)),
            vm((T, 128)), vm((T, 128)), vm((64, T)), vm((T, 128)), vm((128, T)),
            vm((T, 128), F32), vm((ND, 16, 128)), vm((ND, 16, 128)), vm((4, 256, 256)),
            vm((256, D), F32), vm((D, 768), F32), vm((256, D), F32),
            vm((NG, HF, D)), vm((NG, HF, D)), vm((NB, HF, D)), vm((ND, 16, 128)), vm((80, 16, D)),
            vm((ND, 16, 128)), vm((NB, HF, D)),
            vm((W, D)), vm((W, D), F32), vm((D, 256), F32), vm((4, 32, D)), vm((48, 16, 128)),
            vm((4, 32, D)), vm((32, D)), vm((ND, 16, 128)),
            pltpu.SemaphoreType.DMA((11,)), pltpu.SemaphoreType.DMA((11,)), pltpu.SemaphoreType.DMA((3,)),
            pltpu.SemaphoreType.DMA((NP,)), pltpu.SemaphoreType.DMA((NQ,)), pltpu.SemaphoreType.DMA((8,)),
            pltpu.SemaphoreType.DMA((13,)),
        ],
        compiler_params=pltpu.CompilerParams(
            collective_id=1, has_side_effects=True, vmem_limit_bytes=VMEM_LIMIT
        ),
    )(band_widths, spectrum[0], band_weight.reshape(NG * W, D), qkv_time, out_time, qkv_band, out_band,
      cotangent[0], *tables)

    band_grad = out.reshape(NG, W, D).astype(F32)
    return (latent[None], band_grad, share.reshape(-1))


def solution(mesh):
    placed = (
        P(None, "frames", None),
        P(),
        P("bands", None, None),
        P(),
        P(),
        P(),
        P(),
        P(None, "bands", "frames", None),
    )
    return jax.shard_map(
        shards,
        mesh=mesh,
        in_specs=placed,
        out_specs=(
            P(None, "bands", "frames", None),
            P("bands", None, None),
            P(("frames", "bands")),
        ),
        check_vma=False,
    )
```

```python
import math

import jax
import jax.numpy as jnp
import numpy as np
from jax import lax
from jax.experimental import pallas as pl
from jax.experimental.pallas import tpu as pltpu
from jax.sharding import PartitionSpec as P

EPS = 1e-05
THETA = 10000.0
NB = 32
NG = 16
NF = 64
ND = 128
FB = 64
HF = 32
T = 4096
D = 384
W = 128
BQ = 256
NQ = T // BQ
BP = 512
NP = T // BP
CF = 512
CB = 1024
LOG2E = math.log2(math.e)
BF = jnp.bfloat16
F32 = jnp.float32
MESH = pl.DeviceIdType.MESH
VMEM_LIMIT = 63 * 1024 * 1024

NN = (((1,), (0,)), ((), ()))
NT = (((1,), (1,)), ((), ()))
TN = (((0,), (0,)), ((), ()))


def mm(a, b, dims=NN):
    return lax.dot_general(a, b, dims, preferred_element_type=F32)


def lanes(shape):
    return lax.broadcasted_iota(jnp.int32, shape, len(shape) - 1)


def swap_halves(x):
    lane = lanes(x.shape)
    ax = len(x.shape) - 1
    return jnp.where(lane % 64 < 32, pltpu.roll(x, 96, ax), pltpu.roll(x, 32, ax))


def rotary_tables(positions):
    i = np.arange(128) % 32
    freq = np.exp(i.astype(np.float64) * (-2.0 * math.log(THETA) / 64))
    sign = np.where(np.arange(128) % 64 < 32, -1.0, 1.0)
    ang = np.asarray(positions, np.float64)[:, None] * freq[None, :]
    return np.cos(ang).astype(np.float32), (np.sin(ang) * sign).astype(np.float32)


def here():
    return lax.axis_index("frames"), lax.axis_index("bands")


def wait_bytes(ref, sem):
    pltpu.make_async_copy(ref, ref, sem).wait()


def copy_to(src, dst, send_sem, recv_sem, frames, bands):
    pltpu.make_async_remote_copy(
        src, dst, send_sem, recv_sem, device_id=(frames, bands), device_id_type=MESH
    ).start()


def copy_out(src, dst, send_sem, recv_sem, frames, bands):
    fi, bi = here()
    mine = jnp.logical_and(frames == fi, bands == bi)

    @pl.when(mine)
    def _():
        pltpu.make_async_copy(src, dst, recv_sem).start()

    @pl.when(jnp.logical_not(mine))
    def _():
        copy_to(src, dst, send_sem, recv_sem, frames, bands)


def loop(lo, hi, body):
    def step(i, carry):
        body(i)
        return carry

    lax.fori_loop(lo, hi, step, 0)


def rows_of(j, n=BQ):
    return pl.ds(pl.multiple_of(j * n, n), n)


def angles_at(c, cc, sc, cr, sr):
    ca = cc[pl.ds(c, 1), :]
    sa = sc[pl.ds(c, 1), :]
    return ca * cr[...] - sa * sr[...], sa * cr[...] + ca * sr[...]


def normed_rows(feat_rows, bwk):
    lat = mm(feat_rows, bwk).astype(BF).astype(F32)
    r = lax.rsqrt(jnp.mean(lat * lat, axis=-1, keepdims=True) + EPS)
    return lat * r, r


def own_columns(qt, wh):
    head = lax.rem(lax.axis_index("frames"), 4)
    parts = []
    for s in range(3):
        x = qt[:, pl.ds(pl.multiple_of(s * 256 + (head // 2) * 128, 128), 128)].astype(F32)
        parts.append(jnp.where(lax.rem(head, 2) == 1, pltpu.roll(x, 64, 1), x))
    low = lanes((D, 128)) < 64
    wh[:, 0:128] = jnp.where(low, parts[0], pltpu.roll(parts[1], 64, 1)).astype(BF)
    wh[:, 128:256] = jnp.where(low, parts[2], 0.0).astype(BF)


def make_features(widths, spec, bw, feat, lat):
    bi = lax.axis_index("bands")
    start = jnp.int32(0)
    for j in range(NG):
        start = start + jnp.where(bi == 1, widths[j], 0)

    def one(k, start):
        w = widths[bi * NG + k]
        col = lax.broadcasted_iota(jnp.int32, (spec.shape[1], W), 0)
        lane = lanes((spec.shape[1], W))
        pick = jnp.logical_and(col - lane == 2 * start, lane < 2 * w)
        y = mm(spec[...], jnp.where(pick, 1.0, 0.0).astype(BF)).astype(BF)
        feat[k] = y
        lat[k] = mm(y, bw[rows_of(k, W), 0:D]).astype(BF)
        return start + w

    lax.fori_loop(0, NG, one, start)


def project(feat, arrived, bwk, wh, tables, q_s, k_s, kt_s, v_s, vt_s, midway):
    fi, _ = here()

    def pre(i):
        j = lax.rem(fi // 8 + 2 * NP - 1 - i, NP)
        rows = rows_of(j, BP)
        wait_bytes(feat.at[rows_of(j, 8)], arrived.at[j])
        f = feat[rows_of(j, 8)].reshape(BP, W)
        n, _r = normed_rows(f, bwk[...])
        proj = mm(n.astype(BF), wh[...])
        co, si = angles_at(j, *tables)
        a = proj[:, :128]
        a = a * co + swap_halves(a) * si
        low = lanes(a.shape) < 64
        q_s[rows, :] = (a * (0.125 * LOG2E)).astype(BF)
        k = jnp.where(low, pltpu.roll(a, 64, 1), 0.0)
        k_s[rows, :] = k.astype(BF)
        kt_s[:, rows] = k.T[:64].astype(BF)
        v = jnp.where(low, proj[:, 128:], 1.0)
        v_s[rows, :] = v.astype(BF)
        vt_s[:, rows] = v.T.astype(BF)
        pl.when(i == 5)(midway)

    loop(0, NP, pre)


def attend(blk, q_s, kt_s, v_s, e_s, s_s, ol, op):
    rows = rows_of(blk)
    q = q_s[rows, :][:, :64]
    top = jnp.full((BQ, 128), -jnp.inf, F32)
    for j in range(T // CF):
        cols = slice(j * CF, (j + 1) * CF)
        s = mm(q, kt_s[:, cols])
        s_s[:, cols] = s
        for i in range(CF // 128):
            top = jnp.maximum(top, s[:, 128 * i:128 * i + 128])
    top = jnp.max(top, axis=1, keepdims=True)
    res = jnp.zeros((BQ, 128), F32)
    for j in range(T // CF):
        cols = slice(j * CF, (j + 1) * CF)
        e = jnp.exp2(s_s[:, cols] - top).astype(BF)
        e_s[rows, cols] = e
        res = res + mm(e, v_s[cols, :])
    rl = 1.0 / res
    low = lanes(res.shape) < 64
    o = res * pltpu.roll(rl, 64, 1)
    ol[rows, :] = jnp.where(low, o, rl)
    o4 = o.reshape(BQ // HF, 2, 16, 128)
    low3 = lanes((BQ // HF, 16, 128)) < 64
    op[pl.ds(pl.multiple_of(blk * 8, 8), 8)] = jnp.where(low3, o4[:, 0], pltpu.roll(o4[:, 1], 64, 2)).astype(BF)


def attend_back(c, e_s, q_s, k_s, vt_s, ol, dop, t_s):
    rows = rows_of(c)
    x = dop[pl.ds(pl.multiple_of(c * 8, 8), 8)].astype(F32)
    do = jnp.concatenate([x[:, None], pltpu.roll(x, 64, 2)[:, None]], axis=1).reshape(BQ, 128)
    o = ol[rows, :]
    lane = lanes((BQ, 128))
    do = jnp.where(lane < 64, do * pltpu.roll(o, 64, 1), 0.0)
    delta = jnp.sum(do * o, axis=1, keepdims=True)
    hi = delta.astype(BF).astype(F32)
    aug = jnp.where(lane == 64, -hi, jnp.where(lane == 65, hi - delta, do)).astype(BF)
    do_t = do.T[:64].astype(BF)
    q_t = q_s[rows, :].astype(F32).T[:64].astype(BF)
    dq = jnp.zeros((BQ, 128), F32)
    for j in range(T // CB):
        cols = slice(j * CB, (j + 1) * CB)
        e = e_s[rows, cols]
        ds = (e.astype(F32) * mm(aug, vt_s[:, cols])).astype(BF)
        dq = dq + mm(ds, k_s[cols, :])
        t_s[0:64, cols] += mm(do_t, e)
        t_s[64:128, cols] += mm(q_t, ds)
    ol[rows, :] = dq * 0.125


def project_back(feat, bwk, wh, tables, dq_s, t_s, gb_s, dproj_s, n_s):
    low = lanes((BP, 128)) < 64

    def post(j):
        rows = rows_of(j, BP)
        tx = t_s[0:128, rows].T
        a = jnp.where(low, dq_s[rows, :], tx * math.log(2.0)).astype(BF).astype(F32)
        co, si = angles_at(j, *tables)
        a = a * co - swap_halves(a) * si
        dproj = jnp.concatenate([a, jnp.where(low, tx, 0.0)], axis=1).astype(BF)
        dn = mm(dproj, wh[...], NT).astype(BF).astype(F32)
        f = feat[rows_of(j, 8)].reshape(BP, W)
        n, r = normed_rows(f, bwk[...])
        dlat = (r * (dn - n * jnp.mean(n * dn, axis=1, keepdims=True))).astype(BF)
        gb_s[...] += mm(f, dlat, TN)
        dproj_s[rows, :] = dproj
        n_s[rows, :] = n.astype(BF)

    loop(0, NP, post)


def band_layer(lat_all, lat_oth, cot_own, cot_oth, att, w_ot, w_qb, w_ob, cb, sb,
               lat_keep, lat_send, dsec_out, dop_out, wg_out, s_s, att_s, g_ot, g_qb, g_ob, wait_att):
    bi = lax.axis_index("bands")
    own = pl.ds(pl.multiple_of(bi * 128, 128), 128)
    oth = pl.ds(pl.multiple_of((1 - bi) * 128, 128), 128)
    mine = pl.ds(pl.multiple_of(bi * HF, HF), HF)

    def lat_at(g):
        return pl.ds(pl.multiple_of(g * D, 128), D)

    def cot_at(g):
        return pl.ds(pl.multiple_of(4 * D + g * D, 128), D)

    def do_at(g):
        return pl.ds(pl.multiple_of(8 * D + g * 256, 128), 256)

    for x, at, where in ((lat_all[:, mine, :], lat_at, own), (lat_oth[...], lat_at, oth),
                         (cot_own[...], cot_at, own), (cot_oth[...], cot_at, oth)):
        x = x.astype(F32)
        for g in range(4):
            s_s[where, at(g)] = x[:, 8 * g:8 * g + 8, :].reshape(128, D)
    g_ot[...] = jnp.zeros_like(g_ot)
    g_qb[...] = jnp.zeros_like(g_qb)
    g_ob[...] = jnp.zeros_like(g_ob)
    low = lanes((256, 128)) < 64
    wait_att()

    def pair(a, b, p):
        if p == 0:
            return jnp.where(low, a, pltpu.roll(b, 64, 1))
        return jnp.where(low, pltpu.roll(a, 64, 1), b)

    for j in range(2):
        x0 = att[:, 2 * j].astype(F32)
        x1 = att[:, 2 * j + 1].astype(F32)
        for g in range(4):
            p, rr = g // 2, g % 2
            a = x0[:, 8 * rr:8 * rr + 8, :].reshape(256, 128)
            b = x1[:, 8 * rr:8 * rr + 8, :].reshape(256, 128)
            att_s[g, :, 128 * j:128 * j + 128] = pair(a, b, p).astype(BF)

    def group(g):
        att_g = att_s[g]
        cot = s_s[:, cot_at(g)]
        cot_b = cot.astype(BF)
        sec = (s_s[:, lat_at(g)] + mm(att_g, w_ot[...])).astype(BF).astype(F32)
        r = lax.rsqrt(jnp.mean(sec * sec, axis=-1, keepdims=True) + EPS)
        n = sec * r
        nb = n.astype(BF)
        proj = mm(nb, w_qb[...])
        dbatt = mm(cot_b, w_ob[...], NT)
        co, si = cb[...], sb[...]
        row_t = lax.broadcasted_iota(jnp.int32, (256, 256), 0) % 8
        col_t = lax.broadcasted_iota(jnp.int32, (256, 256), 1) % 8
        same = row_t == col_t
        batts, dqs, dks, dvs = [], [], [], []
        for j in range(2):
            q = proj[:, 128 * j:128 * j + 128]
            k = proj[:, 256 + 128 * j:384 + 128 * j]
            v = proj[:, 512 + 128 * j:640 + 128 * j].astype(BF)
            q = ((q * co + swap_halves(q) * si) * 0.125).astype(BF)
            k = (k * co + swap_halves(k) * si).astype(BF)
            do = dbatt[:, 128 * j:128 * j + 128].astype(BF)
            outs = []
            for hh in range(2):
                part = low if hh == 0 else jnp.logical_not(low)
                zero = jnp.zeros((), BF)
                qm = jnp.where(part, q, zero)
                dm = jnp.where(part, do, zero)
                s = jnp.where(same, mm(qm, k, NT), -jnp.inf)
                e = jnp.exp(s - jnp.max(s, axis=1, keepdims=True))
                p = e * (1.0 / jnp.sum(e, axis=1, keepdims=True))
                pb = p.astype(BF)
                pf = pb.astype(F32)
                o = mm(pb, v)
                dp = mm(dm, v, NT)
                ds = (pf * (dp - jnp.sum(pf * dp, axis=1, keepdims=True))).astype(BF)
                outs.append((o, mm(ds, k), mm(ds, q, TN), mm(pb, do, TN)))
            batts.append(jnp.where(low, outs[0][0], outs[1][0]).astype(BF))
            dq = (jnp.where(low, outs[0][1], outs[1][1]) * 0.125).astype(BF).astype(F32)
            dk = jnp.where(low, outs[0][2], outs[1][2]).astype(BF).astype(F32)
            dqs.append((dq * co - swap_halves(dq) * si).astype(BF))
            dks.append((dk * co - swap_halves(dk) * si).astype(BF))
            dvs.append(jnp.where(low, outs[0][3], outs[1][3]).astype(BF))
        batt = jnp.concatenate(batts, axis=1)
        dproj = jnp.concatenate(dqs + dks + dvs, axis=1)
        s_s[:, lat_at(g)] = sec + mm(batt, w_ob[...])
        dn = mm(dproj, w_qb[...], NT).astype(BF).astype(F32)
        dsec = (cot + r * (dn - n * jnp.mean(n * dn, axis=1, keepdims=True))).astype(BF)
        s_s[:, cot_at(g)] = dsec.astype(F32)
        s_s[:, do_at(g)] = mm(dsec, w_ot[...], NT)
        g_ob[...] += mm(batt, cot_b, TN)
        g_qb[...] += mm(nb, dproj, TN)
        g_ot[...] += mm(att_g, dsec, TN)

    loop(0, 4, group)

    for j in range(2):
        for hh in range(2):
            parts = []
            for rr in range(2):
                a = s_s[:, do_at(rr)][:, 128 * j:128 * j + 128]
                b = s_s[:, do_at(2 + rr)][:, 128 * j:128 * j + 128]
                parts.append(pair(a, b, hh).reshape(NB, 8, 128))
            dop_out[:, 2 * j + hh] = jnp.concatenate(parts, axis=1).astype(BF)

    def rest():
        dsec_out[...] = jnp.concatenate(
            [s_s[:, cot_at(g)].reshape(NB, 8, D) for g in range(4)], axis=1
        ).astype(BF)
        for ref, where in ((lat_keep, own), (lat_send, oth)):
            ref[...] = jnp.concatenate(
                [s_s[where, lat_at(g)].reshape(NG, 8, D) for g in range(4)], axis=1
            ).astype(BF)
        wg_out[0:16] = g_ot[...].reshape(16, 16, D).astype(BF)
        wg_out[16:64] = jnp.concatenate(
            [g_qb[:, :D].reshape(48, 8, D), g_qb[:, D:].reshape(48, 8, D)], axis=1
        ).astype(BF)
        wg_out[64:80] = g_ob[...].reshape(16, 16, D).astype(BF)

    return rest


def kernel(widths, spec_h, bw, qt_h, w_ot_h, w_qb_h, w_ob_h, cot, cc_h, sc_h, cr_h, sr_h, cb_h, sb_h,
           latent, out, share,
           spec, qt, w_ot, w_qb, w_ob, cc, sc, cr, sr, cb, sb,
           e_s, s_s, feat_own, feat, lat_all, lat_oth, cot_own, cot_oth, wh, q_s, k_s, kt_s, v_s, vt_s,
           ol, op, att, att_s, g_ot, g_qb, g_ob, lat_keep, lat_send, dsec, dop, wg, dop_r, dsec_r,
           bwk, gb_s, gq_s, gband, gq, quad, part, gq_r, send, recv, local,
           feat_in, dop_in, out_in, staged,
           wg_p, wg_s, wg_r, rows_in, group_in):
    fi, bi = here()
    me = fi * 2 + bi
    slot = bi * NF + fi
    head = lax.rem(fi, 4)
    tables = (cc, sc, cr, sr)
    mine = pl.ds(pl.multiple_of(bi * HF, HF), HF)
    other = pl.ds(pl.multiple_of((1 - bi) * HF, HF), HF)

    barrier = pltpu.get_barrier_semaphore()

    row, col = fi // 8, lax.rem(fi, 8)

    def greet(d):
        in_row = row * 8 + lax.rem(col + d, 8)
        in_col = lax.rem(row + d, 8) * 8 + col
        pl.semaphore_signal(barrier, inc=1, device_id=(in_row, bi), device_id_type=MESH)
        pl.semaphore_signal(barrier, inc=1, device_id=(in_col, bi), device_id_type=MESH)

    loop(1, 8, greet)
    pl.semaphore_signal(barrier, inc=1, device_id=(fi, 1 - bi), device_id_type=MESH)

    bw_at = e_s.at[pl.ds(0, NG * W), pl.ds(0, D)]
    first = ((bw, bw_at), (spec_h, spec), (qt_h, qt))
    later = ((cc_h, cc), (sc_h, sc), (cr_h, cr), (sr_h, sr), (w_ot_h, w_ot), (w_qb_h, w_qb), (w_ob_h, w_ob),
             (cb_h, cb), (sb_h, sb), (cot.at[:, mine, :], cot_own))
    copies = [pltpu.make_async_copy(x, y, staged.at[i]) for i, (x, y) in enumerate(first + later)]
    for c in copies:
        c.start()
    for c in copies[:len(first)]:
        c.wait()
    own_columns(qt, wh)
    make_features(widths, spec, e_s, feat_own, lat_all)
    bwk[...] = e_s[rows_of(fi // 4, W), 0:D]
    for c in copies[len(first):]:
        c.wait()
    pl.semaphore_wait(barrier, 15)

    def greet_again(d):
        in_col = lax.rem(row + d, 8) * 8 + col
        pl.semaphore_signal(rows_in, inc=1, device_id=(in_col, bi), device_id_type=MESH)

    loop(1, 8, greet_again)
    pl.semaphore_wait(rows_in, 7)
    pl.semaphore_signal(group_in, inc=1, device_id=(fi, 1 - bi), device_id_type=MESH)

    pltpu.make_async_copy(feat_own.at[fi // 4], feat.at[fi], feat_in.at[fi // 8]).start()

    def give_features(d):
        t = lax.rem(fi + d, NF)
        copy_to(feat_own.at[t // 4], feat.at[fi], send.at[0], feat_in.at[fi // 8], t, bi)

    loop(1, NF, give_features)

    def give_halves():
        copy_to(cot.at[:, other, :], cot_oth, send.at[2], recv.at[2], fi, 1 - bi)
        copy_to(lat_all.at[:, other, :], lat_oth, send.at[1], recv.at[1], fi, 1 - bi)

    project(feat, feat_in, bwk, wh, tables, q_s, k_s, kt_s, v_s, vt_s, give_halves)
    pl.semaphore_wait(group_in, 1)

    def forward(c):
        blk = lax.rem(c + fi // 4, NQ)
        attend(blk, q_s, kt_s, v_s, e_s, s_s, ol, op)

        def give(u):
            d = blk * 8 + u
            copy_out(op.at[d], att.at[slot], send.at[3], recv.at[3], d // 2, lax.rem(d, 2))

        loop(0, 8, give)

    loop(0, NQ, forward)

    wait_bytes(lat_oth, recv.at[1])
    wait_bytes(cot_oth, recv.at[2])
    rest = band_layer(
        lat_all, lat_oth, cot_own, cot_oth, att.reshape(NB, 4, 16, 128), w_ot, w_qb, w_ob, cb, sb,
        lat_keep, lat_send, dsec, dop.reshape(NB, 4, 16, 128), wg, s_s, att_s, g_ot, g_qb, g_ob,
        lambda: wait_bytes(att, recv.at[3]))

    group = fi // 4
    pltpu.make_async_copy(dop.at[slot], dop_r.at[me], dop_in.at[group]).start()
    copy_to(dop.at[(1 - bi) * NF + fi], dop_r.at[me], send.at[4], dop_in.at[group], fi, 1 - bi)

    def give_back(d):
        f = lax.rem(fi + d, NF)
        copy_to(dop.at[f], dop_r.at[me], send.at[4], dop_in.at[group], f, 0)
        copy_to(dop.at[NF + f], dop_r.at[me], send.at[4], dop_in.at[group], f, 1)

    loop(1, NF, give_back)
    rest()

    quarter = fi // 16
    place = lax.rem(fi, 16) * 2 + bi

    def give_second():
        def one(k):
            copy_out(dsec.at[k], dsec_r.at[place], send.at[5], recv.at[5],
                     lax.rem(k, NG) * 4 + quarter, k // NG)

        loop(0, NB, one)

    def give_latent():
        copy_to(lat_send, latent.at[:, mine, :], send.at[7], recv.at[7], fi, 1 - bi)
        pltpu.make_async_copy(lat_keep, latent.at[:, mine, :], local.at[1]).start()

    def give_weights():
        pltpu.make_async_copy(wg.at[rows_of(col, 10)], wg_p.at[col], recv.at[6]).start()

        def one(d):
            t = lax.rem(col + d, 8)
            copy_to(wg.at[rows_of(t, 10)], wg_p.at[col], send.at[6], recv.at[6], row * 8 + t, bi)

        loop(1, 8, one)

    def give_sums():
        wait_bytes(wg_p, recv.at[6])
        wg_s[...] = jnp.sum(wg_p[...].astype(F32), axis=0).astype(BF)

        def one(u):
            d = 48 + col * 10 + u
            copy_out(wg_s.at[u], wg_r.at[row * 2 + bi], send.at[11], recv.at[11], d // 2, lax.rem(d, 2))

        loop(0, 10, one)

    s_s[0:128, :] = jnp.zeros((128, T), F32)

    def backward(i):
        c = lax.rem(group + 2 * NQ - 1 - i, NQ)
        wait_bytes(dop_r.at[rows_of(c, 8)], dop_in.at[c])
        attend_back(c, e_s, q_s, k_s, vt_s, ol, dop_r, s_s)
        pl.when(i == 3)(give_second)
        pl.when(i == 5)(give_weights)
        pl.when(i == 7)(give_latent)
        pl.when(i == 13)(give_sums)

    loop(0, NQ, backward)

    wait_bytes(dsec_r, recv.at[5])
    f = feat[rows_of(head, 16)].reshape(1024, W)
    gb_s[...] = mm(f, dsec_r[...].reshape(1024, D), TN)
    dproj_s = e_s.at[:, pl.ds(0, 256)]
    n_s = e_s.at[:, pl.ds(256, D)]
    project_back(feat, bwk, wh, tables, ol, s_s, gb_s, dproj_s, n_s)

    gband[...] = gb_s[...].reshape(4, 32, D).astype(BF)
    base = fi - head
    pltpu.make_async_copy(gband.at[head], quad.at[head], recv.at[8]).start()
    for d in range(1, 4):
        t = lax.rem(head + d, 4)
        copy_to(gband.at[t], quad.at[head], send.at[8], recv.at[8], base + t, bi)

    gq_s[...] = jnp.zeros_like(gq_s)

    def weight(j):
        rows = rows_of(j, 1024)
        gq_s[...] += mm(n_s[rows, :], dproj_s[rows, :], TN)

    loop(0, 4, weight)

    chip, core = fi // 2, lax.rem(fi, 2)
    mate = fi + 1 - 2 * core
    wait_bytes(quad, recv.at[8])
    part[...] = jnp.sum(quad[...].astype(F32), axis=0).astype(BF)
    pltpu.make_async_copy(part, out.at[chip, core], out_in.at[chip // 4]).start()

    def give_band(d):
        copy_to(part, out.at[chip, core], send.at[10], out_in.at[chip // 4],
                lax.rem(chip + d, 32) * 2 + core, bi)

    loop(1, 32, give_band)

    g = gq_s[...]
    gq[...] = jnp.concatenate(
        [g[:, :128].reshape(48, 8, 128), g[:, 128:].reshape(48, 8, 128)], axis=1
    ).astype(BF)
    loop(0, 48, lambda d: copy_out(gq.at[d], gq_r.at[me], send.at[9], recv.at[9], d // 2, lax.rem(d, 2)))

    def pass_on(i):
        j = lax.rem(chip // 4 + 15 - i, 8)
        block = out.at[rows_of(j, 4), core]
        wait_bytes(block, out_in.at[j])
        copy_to(block, block, send.at[0], recv.at[10], mate, bi)

    low8 = lanes((8, 128)) < 64

    wait_bytes(feat.at[pl.ds(0, NF - 1)], send.at[0])
    loop(0, 8, pass_on)

    @pl.when(me < 48)
    def _():
        wait_bytes(gq_r, recv.at[9])
        x = jnp.sum(gq_r[...].reshape(NG, 4, 2, 16, 128).astype(F32), axis=(0, 2))
        for j in range(2):
            a, b = x[2 * j], x[2 * j + 1]
            share[pl.ds(j, 8, stride=6), :] = jnp.where(low8, a[:8], pltpu.roll(b[:8], 64, 1))
            share[pl.ds(2 + j, 8, stride=6), :] = jnp.where(low8, pltpu.roll(a[:8], 64, 1), b[:8])
            share[pl.ds(4 + j, 8, stride=6), :] = jnp.where(low8, a[8:], pltpu.roll(b[8:], 64, 1))

    @pl.when(me >= 48)
    def _():
        wait_bytes(wg_r, recv.at[11])
        x = jnp.sum(wg_r[...].astype(F32), axis=0)
        wide = jnp.logical_and(me >= 64, me < 112)

        @pl.when(wide)
        def _():
            for j in range(3):
                share[pl.ds(j, 8, stride=6), :] = x[:8, 128 * j:128 * j + 128]
                share[pl.ds(3 + j, 8, stride=6), :] = x[8:, 128 * j:128 * j + 128]

        @pl.when(jnp.logical_not(wide))
        def _():
            for j in range(3):
                share[pl.ds(j, 16, stride=3), :] = x[:, 128 * j:128 * j + 128]

    wait_bytes(latent.at[:, other, :], recv.at[7])
    pltpu.make_async_copy(lat_keep, latent.at[:, mine, :], local.at[1]).wait()
    wait_bytes(out.at[:, 1 - core], recv.at[10])
    wait_bytes(out.at[:, core], send.at[0])
    wait_bytes(lat_oth, send.at[1])
    wait_bytes(cot_oth, send.at[2])
    wait_bytes(op.at[pl.ds(0, ND - 1)], send.at[3])
    wait_bytes(dop.at[pl.ds(0, ND - 1)], send.at[4])
    wait_bytes(dsec.at[pl.ds(0, NB - 1)], send.at[5])
    wait_bytes(lat_send, send.at[7])
    wait_bytes(gband.at[pl.ds(0, 3)], send.at[8])
    wait_bytes(gq.at[pl.ds(0, 47)], send.at[9])
    wait_bytes(wg.at[pl.ds(0, 70)], send.at[6])
    wait_bytes(wg_s.at[pl.ds(0, 9)], send.at[11])
    wait_bytes(out.at[pl.ds(0, 31), core], send.at[10])

    @pl.when(head != quarter)
    def _():
        wait_bytes(dsec.at[0], send.at[5])

    @pl.when(me >= 48)
    def _():
        wait_bytes(gq.at[0], send.at[9])

    @pl.when(jnp.logical_or(me < 48, (me - 48) // 10 != col))
    def _():
        wait_bytes(wg_s.at[0], send.at[11])


VM = pl.BlockSpec(memory_space=pltpu.VMEM)
SM = pl.BlockSpec(memory_space=pltpu.SMEM)
ANY = pl.BlockSpec(memory_space=pl.ANY)


def struct(shape, dtype):
    return jax.ShapeDtypeStruct(shape, dtype)


def shards(spectrum, band_widths, band_weight, qkv_time, out_time, qkv_band, out_band, cotangent):
    tables = rotary_tables(np.arange(NP) * BP) + rotary_tables(np.arange(BP)) + rotary_tables(np.arange(256) // 8)
    tables = tuple(jnp.asarray(x) for x in tables)

    def vm(shape, dtype=BF):
        return pltpu.VMEM(shape, dtype)

    latent, out, share = pl.pallas_call(
        kernel,
        out_shape=[struct((NG, FB, D), BF), struct((32, 2, 32, D), BF), struct((48, 128), F32)],
        in_specs=[SM] + [ANY] * 13,
        out_specs=[ANY, ANY, VM],
        scratch_shapes=[
            vm((FB, 1280)), vm((D, 768)), vm((256, D)), vm((D, 768)), vm((256, D)),
            vm((NP, 128), F32), vm((NP, 128), F32), vm((BP, 128), F32), vm((BP, 128), F32),
            vm((256, 128), F32), vm((256, 128), F32),
            vm((T, T)), vm((BQ, T), F32), vm((NG, FB, W)), vm((NF, FB, W)), vm((NG, FB, D)),
            vm((NG, HF, D)), vm((NG, HF, D)), vm((NG, HF, D)), vm((D, 256)),
            vm((T, 128)), vm((T, 128)), vm((64, T)), vm((T, 128)), vm((128, T)),
            vm((T, 128), F32), vm((ND, 16, 128)), vm((ND, 16, 128)), vm((4, 256, 256)),
            vm((256, D), F32), vm((D, 768), F32), vm((256, D), F32),
            vm((NG, HF, D)), vm((NG, HF, D)), vm((NB, HF, D)), vm((ND, 16, 128)), vm((80, 16, D)),
            vm((ND, 16, 128)), vm((NB, HF, D)),
            vm((W, D)), vm((W, D), F32), vm((D, 256), F32), vm((4, 32, D)), vm((48, 16, 128)),
            vm((4, 32, D)), vm((32, D)), vm((ND, 16, 128)),
            pltpu.SemaphoreType.DMA((12,)), pltpu.SemaphoreType.DMA((12,)), pltpu.SemaphoreType.DMA((3,)),
            pltpu.SemaphoreType.DMA((NP,)), pltpu.SemaphoreType.DMA((NQ,)), pltpu.SemaphoreType.DMA((8,)),
            pltpu.SemaphoreType.DMA((13,)),
            vm((8, 10, 16, D)), vm((10, 16, D)), vm((16, 16, D)),
            pltpu.SemaphoreType.REGULAR, pltpu.SemaphoreType.REGULAR,
        ],
        compiler_params=pltpu.CompilerParams(
            collective_id=1, has_side_effects=True, vmem_limit_bytes=VMEM_LIMIT
        ),
    )(band_widths, spectrum[0], band_weight.reshape(NG * W, D), qkv_time, out_time, qkv_band, out_band,
      cotangent[0], *tables)

    band_grad = out.reshape(NG, W, D).astype(F32)
    return (latent[None], band_grad, share.reshape(-1))


def solution(mesh):
    placed = (
        P(None, "frames", None),
        P(),
        P("bands", None, None),
        P(),
        P(),
        P(),
        P(),
        P(None, "bands", "frames", None),
    )
    return jax.shard_map(
        shards,
        mesh=mesh,
        in_specs=placed,
        out_specs=(
            P(None, "bands", "frames", None),
            P("bands", None, None),
            P(("frames", "bands")),
        ),
        check_vma=False,
    )
```

```python
import math

import jax
import jax.numpy as jnp
import numpy as np
from jax import lax
from jax.experimental import pallas as pl
from jax.experimental.pallas import tpu as pltpu
from jax.sharding import PartitionSpec as P

EPS = 1e-05
THETA = 10000.0
NB = 32
NG = 16
NF = 64
ND = 128
FB = 64
HF = 32
T = 4096
D = 384
W = 128
BQ = 256
NQ = T // BQ
BP = 512
NP = T // BP
CF = 512
CB = 1024
LOG2E = math.log2(math.e)
BF = jnp.bfloat16
F32 = jnp.float32
MESH = pl.DeviceIdType.MESH
VMEM_LIMIT = 63 * 1024 * 1024

NN = (((1,), (0,)), ((), ()))
NT = (((1,), (1,)), ((), ()))
TN = (((0,), (0,)), ((), ()))


def mm(a, b, dims=NN):
    return lax.dot_general(a, b, dims, preferred_element_type=F32)


def lanes(shape):
    return lax.broadcasted_iota(jnp.int32, shape, len(shape) - 1)


def swap_halves(x):
    lane = lanes(x.shape)
    ax = len(x.shape) - 1
    return jnp.where(lane % 64 < 32, pltpu.roll(x, 96, ax), pltpu.roll(x, 32, ax))


def rotary_tables(positions):
    i = np.arange(128) % 32
    freq = np.exp(i.astype(np.float64) * (-2.0 * math.log(THETA) / 64))
    sign = np.where(np.arange(128) % 64 < 32, -1.0, 1.0)
    ang = np.asarray(positions, np.float64)[:, None] * freq[None, :]
    return np.cos(ang).astype(np.float32), (np.sin(ang) * sign).astype(np.float32)


def here():
    return lax.axis_index("frames"), lax.axis_index("bands")


def wait_bytes(ref, sem):
    pltpu.make_async_copy(ref, ref, sem).wait()


def copy_to(src, dst, send_sem, recv_sem, frames, bands):
    pltpu.make_async_remote_copy(
        src, dst, send_sem, recv_sem, device_id=(frames, bands), device_id_type=MESH
    ).start()


def copy_out(src, dst, send_sem, recv_sem, frames, bands):
    fi, bi = here()
    mine = jnp.logical_and(frames == fi, bands == bi)

    @pl.when(mine)
    def _():
        pltpu.make_async_copy(src, dst, recv_sem).start()

    @pl.when(jnp.logical_not(mine))
    def _():
        copy_to(src, dst, send_sem, recv_sem, frames, bands)


def loop(lo, hi, body):
    def step(i, carry):
        body(i)
        return carry

    lax.fori_loop(lo, hi, step, 0)


def rows_of(j, n=BQ):
    return pl.ds(pl.multiple_of(j * n, n), n)


def angles_at(c, cc, sc, cr, sr):
    ca = cc[pl.ds(c, 1), :]
    sa = sc[pl.ds(c, 1), :]
    return ca * cr[...] - sa * sr[...], sa * cr[...] + ca * sr[...]


def normed_rows(feat_rows, bwk):
    lat = mm(feat_rows, bwk).astype(BF).astype(F32)
    r = lax.rsqrt(jnp.mean(lat * lat, axis=-1, keepdims=True) + EPS)
    return lat * r, r


def own_columns(qt, wh):
    head = lax.rem(lax.axis_index("frames"), 4)
    parts = []
    for s in range(3):
        x = qt[:, pl.ds(pl.multiple_of(s * 256 + (head // 2) * 128, 128), 128)].astype(F32)
        parts.append(jnp.where(lax.rem(head, 2) == 1, pltpu.roll(x, 64, 1), x))
    low = lanes((D, 128)) < 64
    wh[:, 0:128] = jnp.where(low, parts[0], pltpu.roll(parts[1], 64, 1)).astype(BF)
    wh[:, 128:256] = jnp.where(low, parts[2], 0.0).astype(BF)


def make_features(widths, spec, bw, feat, lat):
    bi = lax.axis_index("bands")
    start = jnp.int32(0)
    for j in range(NG):
        start = start + jnp.where(bi == 1, widths[j], 0)

    lane = lanes((256, W))
    diff = lax.broadcasted_iota(jnp.int32, (256, W), 0) - lane

    def one(k, start):
        w = widths[bi * NG + k]
        blk = (2 * start) // 128
        a = spec[:, 0:128]
        b = spec[:, 128:256]
        last = spec.shape[1] // 128 - 1
        for n in range(1, last + 1):
            a = jnp.where(blk == n, spec[:, 128 * n:128 * n + 128], a)
        for n in range(2, last + 1):
            b = jnp.where(blk == n - 1, spec[:, 128 * n:128 * n + 128], b)
        pick = jnp.logical_and(diff == 2 * start - 128 * blk, lane < 2 * w)
        y = mm(jnp.concatenate([a, b], axis=1), jnp.where(pick, 1.0, 0.0).astype(BF)).astype(BF)
        feat[k] = y
        lat[k] = mm(y, bw[rows_of(k, W), 0:D]).astype(BF)
        return start + w

    lax.fori_loop(0, NG, one, start)


def project(feat, step, bwk, wh, tables, q_s, k_s, kt_s, v_s, vt_s):
    def pre(j):
        rows = rows_of(j, BP)
        f = feat[rows_of(j, 8)].reshape(BP, W)
        n, _r = normed_rows(f, bwk[...])
        proj = mm(n.astype(BF), wh[...])
        co, si = angles_at(j, *tables)
        a = proj[:, :128]
        a = a * co + swap_halves(a) * si
        low = lanes(a.shape) < 64
        q_s[rows, :] = (a * (0.125 * LOG2E)).astype(BF)
        k = jnp.where(low, pltpu.roll(a, 64, 1), 0.0)
        k_s[rows, :] = k.astype(BF)
        kt_s[:, rows] = k.T[:64].astype(BF)
        v = jnp.where(low, proj[:, 128:], 1.0)
        v_s[rows, :] = v.astype(BF)
        vt_s[:, rows] = v.T.astype(BF)

    def quarter(i):
        at = step(i)
        loop(0, 2, lambda u: pre(2 * at + u))

    loop(0, 4, quarter)


def attend(blk, q_s, kt_s, v_s, e_s, s_s, ol, op):
    rows = rows_of(blk)
    q = q_s[rows, :][:, :64]
    top = jnp.full((BQ, 128), -jnp.inf, F32)
    for j in range(T // CF):
        cols = slice(j * CF, (j + 1) * CF)
        s = mm(q, kt_s[:, cols])
        s_s[:, cols] = s
        for i in range(CF // 128):
            top = jnp.maximum(top, s[:, 128 * i:128 * i + 128])
    top = jnp.max(top, axis=1, keepdims=True)
    res = jnp.zeros((BQ, 128), F32)
    for j in range(T // CF):
        cols = slice(j * CF, (j + 1) * CF)
        e = jnp.exp2(s_s[:, cols] - top).astype(BF)
        e_s[rows, cols] = e
        res = res + mm(e, v_s[cols, :])
    rl = 1.0 / res
    low = lanes(res.shape) < 64
    o = res * pltpu.roll(rl, 64, 1)
    ol[rows, :] = jnp.where(low, o, rl)
    o4 = o.reshape(BQ // HF, 2, 16, 128)
    low3 = lanes((BQ // HF, 16, 128)) < 64
    op[pl.ds(pl.multiple_of(blk * 8, 8), 8)] = jnp.where(low3, o4[:, 0], pltpu.roll(o4[:, 1], 64, 2)).astype(BF)


def attend_back(c, e_s, q_s, k_s, vt_s, ol, dop, t_s):
    rows = rows_of(c)
    x = dop[pl.ds(pl.multiple_of(c * 8, 8), 8)].astype(F32)
    do = jnp.concatenate([x[:, None], pltpu.roll(x, 64, 2)[:, None]], axis=1).reshape(BQ, 128)
    o = ol[rows, :]
    lane = lanes((BQ, 128))
    do = jnp.where(lane < 64, do * pltpu.roll(o, 64, 1), 0.0)
    delta = jnp.sum(do * o, axis=1, keepdims=True)
    hi = delta.astype(BF).astype(F32)
    aug = jnp.where(lane == 64, -hi, jnp.where(lane == 65, hi - delta, do)).astype(BF)
    do_t = do.T[:64].astype(BF)
    q_t = q_s[rows, :].astype(F32).T[:64].astype(BF)
    dq = jnp.zeros((BQ, 128), F32)
    for j in range(T // CB):
        cols = slice(j * CB, (j + 1) * CB)
        e = e_s[rows, cols]
        ds = (e.astype(F32) * mm(aug, vt_s[:, cols])).astype(BF)
        dq = dq + mm(ds, k_s[cols, :])
        t_s[0:64, cols] += mm(do_t, e)
        t_s[64:128, cols] += mm(q_t, ds)
    ol[rows, :] = dq * 0.125


def project_back(feat, bwk, wh, tables, dq_s, t_s, gb_s, dproj_s, n_s):
    low = lanes((BP, 128)) < 64

    def post(j):
        rows = rows_of(j, BP)
        tx = t_s[0:128, rows].T
        a = jnp.where(low, dq_s[rows, :], tx * math.log(2.0)).astype(BF).astype(F32)
        co, si = angles_at(j, *tables)
        a = a * co - swap_halves(a) * si
        dproj = jnp.concatenate([a, jnp.where(low, tx, 0.0)], axis=1).astype(BF)
        dn = mm(dproj, wh[...], NT).astype(BF).astype(F32)
        f = feat[rows_of(j, 8)].reshape(BP, W)
        n, r = normed_rows(f, bwk[...])
        dlat = (r * (dn - n * jnp.mean(n * dn, axis=1, keepdims=True))).astype(BF)
        gb_s[...] += mm(f, dlat, TN)
        dproj_s[rows, :] = dproj
        n_s[rows, :] = n.astype(BF)

    loop(0, NP, post)


def band_layer(lat_all, lat_oth, cot_own, cot_oth, att, w_ot, w_qb, w_ob, cb, sb,
               lat_keep, lat_send, dsec_out, dop_out, wg_out, s_s, att_s, g_ot, g_qb, g_ob, wait_att):
    bi = lax.axis_index("bands")
    own = pl.ds(pl.multiple_of(bi * 128, 128), 128)
    oth = pl.ds(pl.multiple_of((1 - bi) * 128, 128), 128)
    mine = pl.ds(pl.multiple_of(bi * HF, HF), HF)

    def lat_at(g):
        return pl.ds(pl.multiple_of(g * D, 128), D)

    def cot_at(g):
        return pl.ds(pl.multiple_of(4 * D + g * D, 128), D)

    def do_at(g):
        return pl.ds(pl.multiple_of(8 * D + g * 256, 128), 256)

    for x, at, where in ((lat_all[:, mine, :], lat_at, own), (lat_oth[...], lat_at, oth),
                         (cot_own[...], cot_at, own), (cot_oth[...], cot_at, oth)):
        x = x.astype(F32)
        for g in range(4):
            s_s[where, at(g)] = x[:, 8 * g:8 * g + 8, :].reshape(128, D)
    g_ot[...] = jnp.zeros_like(g_ot)
    g_qb[...] = jnp.zeros_like(g_qb)
    g_ob[...] = jnp.zeros_like(g_ob)
    low = lanes((256, 128)) < 64
    wait_att()

    def pair(a, b, p):
        if p == 0:
            return jnp.where(low, a, pltpu.roll(b, 64, 1))
        return jnp.where(low, pltpu.roll(a, 64, 1), b)

    for j in range(2):
        x0 = att[:, 2 * j].astype(F32)
        x1 = att[:, 2 * j + 1].astype(F32)
        for g in range(4):
            p, rr = g // 2, g % 2
            a = x0[:, 8 * rr:8 * rr + 8, :].reshape(256, 128)
            b = x1[:, 8 * rr:8 * rr + 8, :].reshape(256, 128)
            att_s[g, :, 128 * j:128 * j + 128] = pair(a, b, p).astype(BF)

    def group(g):
        att_g = att_s[g]
        cot = s_s[:, cot_at(g)]
        cot_b = cot.astype(BF)
        sec = (s_s[:, lat_at(g)] + mm(att_g, w_ot[...])).astype(BF).astype(F32)
        r = lax.rsqrt(jnp.mean(sec * sec, axis=-1, keepdims=True) + EPS)
        n = sec * r
        nb = n.astype(BF)
        proj = mm(nb, w_qb[...])
        dbatt = mm(cot_b, w_ob[...], NT)
        co, si = cb[...], sb[...]
        row_t = lax.broadcasted_iota(jnp.int32, (256, 256), 0) % 8
        col_t = lax.broadcasted_iota(jnp.int32, (256, 256), 1) % 8
        same = row_t == col_t
        batts, dqs, dks, dvs = [], [], [], []
        for j in range(2):
            q = proj[:, 128 * j:128 * j + 128]
            k = proj[:, 256 + 128 * j:384 + 128 * j]
            v = proj[:, 512 + 128 * j:640 + 128 * j].astype(BF)
            q = ((q * co + swap_halves(q) * si) * 0.125).astype(BF)
            k = (k * co + swap_halves(k) * si).astype(BF)
            do = dbatt[:, 128 * j:128 * j + 128].astype(BF)
            outs = []
            for hh in range(2):
                part = low if hh == 0 else jnp.logical_not(low)
                zero = jnp.zeros((), BF)
                qm = jnp.where(part, q, zero)
                dm = jnp.where(part, do, zero)
                s = jnp.where(same, mm(qm, k, NT), -jnp.inf)
                e = jnp.exp(s - jnp.max(s, axis=1, keepdims=True))
                p = e * (1.0 / jnp.sum(e, axis=1, keepdims=True))
                pb = p.astype(BF)
                pf = pb.astype(F32)
                o = mm(pb, v)
                dp = mm(dm, v, NT)
                ds = (pf * (dp - jnp.sum(pf * dp, axis=1, keepdims=True))).astype(BF)
                outs.append((o, mm(ds, k), mm(ds, q, TN), mm(pb, do, TN)))
            batts.append(jnp.where(low, outs[0][0], outs[1][0]).astype(BF))
            dq = (jnp.where(low, outs[0][1], outs[1][1]) * 0.125).astype(BF).astype(F32)
            dk = jnp.where(low, outs[0][2], outs[1][2]).astype(BF).astype(F32)
            dqs.append((dq * co - swap_halves(dq) * si).astype(BF))
            dks.append((dk * co - swap_halves(dk) * si).astype(BF))
            dvs.append(jnp.where(low, outs[0][3], outs[1][3]).astype(BF))
        batt = jnp.concatenate(batts, axis=1)
        dproj = jnp.concatenate(dqs + dks + dvs, axis=1)
        s_s[:, lat_at(g)] = sec + mm(batt, w_ob[...])
        dn = mm(dproj, w_qb[...], NT).astype(BF).astype(F32)
        dsec = (cot + r * (dn - n * jnp.mean(n * dn, axis=1, keepdims=True))).astype(BF)
        s_s[:, cot_at(g)] = dsec.astype(F32)
        s_s[:, do_at(g)] = mm(dsec, w_ot[...], NT)
        g_ob[...] += mm(batt, cot_b, TN)
        g_qb[...] += mm(nb, dproj, TN)
        g_ot[...] += mm(att_g, dsec, TN)

    loop(0, 4, group)

    for j in range(2):
        for hh in range(2):
            parts = []
            for rr in range(2):
                a = s_s[:, do_at(rr)][:, 128 * j:128 * j + 128]
                b = s_s[:, do_at(2 + rr)][:, 128 * j:128 * j + 128]
                parts.append(pair(a, b, hh).reshape(NB, 8, 128))
            dop_out[:, 2 * j + hh] = jnp.concatenate(parts, axis=1).astype(BF)

    def rest():
        dsec_out[...] = jnp.concatenate(
            [s_s[:, cot_at(g)].reshape(NB, 8, D) for g in range(4)], axis=1
        ).astype(BF)
        for ref, where in ((lat_keep, own), (lat_send, oth)):
            ref[...] = jnp.concatenate(
                [s_s[where, lat_at(g)].reshape(NG, 8, D) for g in range(4)], axis=1
            ).astype(BF)
        wg_out[0:16] = g_ot[...].reshape(16, 16, D).astype(BF)
        wg_out[16:64] = jnp.concatenate(
            [g_qb[:, :D].reshape(48, 8, D), g_qb[:, D:].reshape(48, 8, D)], axis=1
        ).astype(BF)
        wg_out[64:80] = g_ob[...].reshape(16, 16, D).astype(BF)

    return rest


def kernel(widths, spec_h, bw, qt_h, w_ot_h, w_qb_h, w_ob_h, cot, cc_h, sc_h, cr_h, sr_h, cb_h, sb_h,
           latent, out, share,
           spec, qt, w_ot, w_qb, w_ob, cc, sc, cr, sr, cb, sb,
           e_s, s_s, feat_own, feat, lat_all, lat_oth, cot_own, cot_oth, wh, q_s, k_s, kt_s, v_s, vt_s,
           ol, op, att, att_s, g_ot, g_qb, g_ob, dsec, dop, wg, dop_r, dsec_r,
           bwk, gb_s, gq_s, gband, gq, quad, part, gq_r, send, recv, local,
           feat_in, dop_in, out_in, staged,
           wg_p, wg_s, wg_r, rows_in, group_in):
    fi, bi = here()
    me = fi * 2 + bi
    slot = bi * NF + fi
    head = lax.rem(fi, 4)
    tables = (cc, sc, cr, sr)
    mine = pl.ds(pl.multiple_of(bi * HF, HF), HF)
    other = pl.ds(pl.multiple_of((1 - bi) * HF, HF), HF)

    barrier = pltpu.get_barrier_semaphore()

    row, col = fi // 8, lax.rem(fi, 8)

    def greet(d):
        in_row = row * 8 + lax.rem(col + d, 8)
        in_col = lax.rem(row + d, 8) * 8 + col
        pl.semaphore_signal(barrier, inc=1, device_id=(in_row, bi), device_id_type=MESH)
        pl.semaphore_signal(barrier, inc=1, device_id=(in_col, bi), device_id_type=MESH)

    loop(1, 8, greet)
    pl.semaphore_signal(barrier, inc=1, device_id=(fi, 1 - bi), device_id_type=MESH)

    bw_at = e_s.at[pl.ds(0, NG * W), pl.ds(0, D)]
    first = ((bw, bw_at), (spec_h, spec), (qt_h, qt))
    later = ((cc_h, cc), (sc_h, sc), (cr_h, cr), (sr_h, sr), (w_ot_h, w_ot), (w_qb_h, w_qb), (w_ob_h, w_ob),
             (cb_h, cb), (sb_h, sb), (cot.at[:, mine, :], cot_own))
    copies = [pltpu.make_async_copy(x, y, staged.at[i]) for i, (x, y) in enumerate(first + later)]
    for c in copies:
        c.start()
    for c in copies[:len(first)]:
        c.wait()
    own_columns(qt, wh)
    make_features(widths, spec, e_s, feat_own, lat_all)
    bwk[...] = e_s[rows_of(fi // 4, W), 0:D]
    for c in copies[len(first):]:
        c.wait()
    pl.semaphore_wait(barrier, 15)

    def greet_again(d):
        in_col = lax.rem(row + d, 8) * 8 + col
        pl.semaphore_signal(rows_in, inc=1, device_id=(in_col, bi), device_id_type=MESH)

    loop(1, 8, greet_again)
    pl.semaphore_wait(rows_in, 7)
    pl.semaphore_signal(group_in, inc=1, device_id=(fi, 1 - bi), device_id_type=MESH)

    quarter = fi // 16

    def give_features(d):
        k = lax.rem(fi + d, NG)
        copy_out(feat_own.at[k], feat.at[fi], send.at[0], feat_in.at[0, lax.rem(fi, 16) // 4], 4 * k + quarter, bi)

    loop(0, NG, give_features)
    mate = fi + 1 - 2 * lax.rem(fi, 2)
    near = fi + 2 - 4 * lax.rem(fi // 2, 2)

    def give_halves():
        copy_to(cot.at[:, other, :], cot_oth, send.at[2], recv.at[2], fi, 1 - bi)
        copy_to(lat_all.at[:, other, :], lat_oth, send.at[1], recv.at[1], fi, 1 - bi)

    def part_of(quarter, q):
        return feat.at[pl.ds(pl.multiple_of(quarter * 16 + q * 4, 4), 4)]

    def spread(q):
        block = part_of(head, q)
        wait_bytes(block, feat_in.at[0, q])
        copy_to(block, block, send.at[12], feat_in.at[1, q], mate, bi)
        copy_to(block, block, send.at[12], feat_in.at[2, q], near, bi)

    loop(0, 4, spread)

    def step(i):
        at = 2 * lax.rem(head // 2 + i // 2, 2) + lax.rem(head + i, 2)

        @pl.when(i == 1)
        def _():
            give_halves()

        @pl.when(i == 2)
        def _():
            def forward_on(q):
                block = part_of(at, q)
                wait_bytes(block, feat_in.at[2, q])
                copy_to(block, block, send.at[12], feat_in.at[3, q], mate, bi)

            loop(0, 4, forward_on)

        @pl.when(lax.rem(i, 2) == 1)
        def _():
            loop(0, 4, lambda q: wait_bytes(part_of(at, q), feat_in.at[i, q]))

        return at

    project(feat, step, bwk, wh, tables, q_s, k_s, kt_s, v_s, vt_s)
    pl.semaphore_wait(group_in, 1)

    def give_block(blk):
        for u in range(8):
            d = blk * 8 + u
            self_here = d == me
            copy_to(op.at[d], att.at[jnp.where(self_here, (1 - bi) * NF + fi, slot)], send.at[3], recv.at[3],
                    jnp.where(self_here, fi, d // 2), jnp.where(self_here, 1 - bi, lax.rem(d, 2)))

    first_blk = fi // 4
    attend(first_blk, q_s, kt_s, v_s, e_s, s_s, ol, op)

    def forward(c):
        give_block(lax.rem(c + first_blk + NQ - 1, NQ))
        attend(lax.rem(c + first_blk, NQ), q_s, kt_s, v_s, e_s, s_s, ol, op)

    loop(1, NQ, forward)
    give_block(lax.rem(first_blk + NQ - 1, NQ))

    def wait_att():
        wait_bytes(att, recv.at[3])
        att[slot] = op[me]

    wait_bytes(lat_oth, recv.at[1])
    wait_bytes(cot_oth, recv.at[2])
    rest = band_layer(
        lat_all, lat_oth, cot_own, cot_oth, att.reshape(NB, 4, 16, 128), w_ot, w_qb, w_ob, cb, sb,
        cot_own, cot_oth, dsec, dop.reshape(NB, 4, 16, 128), wg, s_s, att_s, g_ot, g_qb, g_ob,
        wait_att)

    group = fi // 4
    pltpu.make_async_copy(dop.at[slot], dop_r.at[me], dop_in.at[group]).start()
    copy_to(dop.at[(1 - bi) * NF + fi], dop_r.at[me], send.at[4], dop_in.at[group], fi, 1 - bi)

    def give_back(d):
        f = lax.rem(fi + d, NF)
        copy_to(dop.at[f], dop_r.at[me], send.at[4], dop_in.at[group], f, 0)
        copy_to(dop.at[NF + f], dop_r.at[me], send.at[4], dop_in.at[group], f, 1)

    loop(1, NF, give_back)
    rest()

    place = lax.rem(fi, 16) * 2 + bi

    def give_second():
        def one(k):
            copy_out(dsec.at[k], dsec_r.at[place], send.at[5], recv.at[5],
                     lax.rem(k, NG) * 4 + quarter, k // NG)

        loop(0, NB, one)

    def give_latent():
        copy_to(cot_oth, latent.at[:, mine, :], send.at[7], recv.at[7], fi, 1 - bi)
        pltpu.make_async_copy(cot_own, latent.at[:, mine, :], local.at[1]).start()

    def give_weights():
        pltpu.make_async_copy(wg.at[rows_of(col, 10)], wg_p.at[col], recv.at[6]).start()

        def one(d):
            t = lax.rem(col + d, 8)
            copy_to(wg.at[rows_of(t, 10)], wg_p.at[col], send.at[6], recv.at[6], row * 8 + t, bi)

        loop(1, 8, one)

    def give_sums():
        wait_bytes(wg_p, recv.at[6])
        wg_s[...] = jnp.sum(wg_p[...].astype(F32), axis=0).astype(BF)

        def one(u):
            d = 48 + col * 10 + u
            copy_out(wg_s.at[u], wg_r.at[row * 2 + bi], send.at[11], recv.at[11], d // 2, lax.rem(d, 2))

        loop(0, 10, one)

    s_s[0:128, :] = jnp.zeros((128, T), F32)

    def backward(i):
        c = lax.rem(group + 2 * NQ - 1 - i, NQ)
        wait_bytes(dop_r.at[rows_of(c, 8)], dop_in.at[c])
        attend_back(c, e_s, q_s, k_s, vt_s, ol, dop_r, s_s)
        pl.when(i == 3)(give_second)
        pl.when(i == 5)(give_weights)
        pl.when(i == 7)(give_latent)
        pl.when(i == 13)(give_sums)

    loop(0, NQ, backward)

    wait_bytes(dsec_r, recv.at[5])
    f = feat[rows_of(head, 16)].reshape(1024, W)
    gb_s[...] = mm(f, dsec_r[...].reshape(1024, D), TN)
    dproj_s = e_s.at[:, pl.ds(0, 256)]
    n_s = e_s.at[:, pl.ds(256, D)]
    project_back(feat, bwk, wh, tables, ol, s_s, gb_s, dproj_s, n_s)

    gband[...] = gb_s[...].reshape(4, 32, D).astype(BF)
    base = fi - head
    pltpu.make_async_copy(gband.at[head], quad.at[head], recv.at[8]).start()
    for d in range(1, 4):
        t = lax.rem(head + d, 4)
        copy_to(gband.at[t], quad.at[head], send.at[8], recv.at[8], base + t, bi)

    gq_s[...] = jnp.zeros_like(gq_s)

    def weight(j):
        rows = rows_of(j, 1024)
        gq_s[...] += mm(n_s[rows, :], dproj_s[rows, :], TN)

    loop(0, 4, weight)

    chip, core = fi // 2, lax.rem(fi, 2)
    wait_bytes(quad, recv.at[8])
    part[...] = jnp.sum(quad[...].astype(F32), axis=0).astype(BF)
    pltpu.make_async_copy(part, out.at[chip, core], out_in.at[chip // 4]).start()

    def give_band(d):
        copy_to(part, out.at[chip, core], send.at[10], out_in.at[chip // 4],
                lax.rem(chip + d, 32) * 2 + core, bi)

    loop(1, 32, give_band)

    g = gq_s[...]
    gq[...] = jnp.concatenate(
        [g[:, :128].reshape(48, 8, 128), g[:, 128:].reshape(48, 8, 128)], axis=1
    ).astype(BF)
    loop(0, 48, lambda d: copy_out(gq.at[d], gq_r.at[me], send.at[9], recv.at[9], d // 2, lax.rem(d, 2)))

    def pass_on(i):
        j = lax.rem(chip // 4 + 15 - i, 8)
        block = out.at[rows_of(j, 4), core]
        wait_bytes(block, out_in.at[j])
        copy_to(block, block, send.at[13], recv.at[10], mate, bi)

    low8 = lanes((8, 128)) < 64

    loop(0, 8, pass_on)

    @pl.when(me < 48)
    def _():
        wait_bytes(gq_r, recv.at[9])
        x = jnp.sum(gq_r[...].reshape(NG, 4, 2, 16, 128).astype(F32), axis=(0, 2))
        for j in range(2):
            a, b = x[2 * j], x[2 * j + 1]
            share[pl.ds(j, 8, stride=6), :] = jnp.where(low8, a[:8], pltpu.roll(b[:8], 64, 1))
            share[pl.ds(2 + j, 8, stride=6), :] = jnp.where(low8, pltpu.roll(a[:8], 64, 1), b[:8])
            share[pl.ds(4 + j, 8, stride=6), :] = jnp.where(low8, a[8:], pltpu.roll(b[8:], 64, 1))

    @pl.when(me >= 48)
    def _():
        wait_bytes(wg_r, recv.at[11])
        x = jnp.sum(wg_r[...].astype(F32), axis=0)
        wide = jnp.logical_and(me >= 64, me < 112)

        @pl.when(wide)
        def _():
            for j in range(3):
                share[pl.ds(j, 8, stride=6), :] = x[:8, 128 * j:128 * j + 128]
                share[pl.ds(3 + j, 8, stride=6), :] = x[8:, 128 * j:128 * j + 128]

        @pl.when(jnp.logical_not(wide))
        def _():
            for j in range(3):
                share[pl.ds(j, 16, stride=3), :] = x[:, 128 * j:128 * j + 128]

    wait_bytes(latent.at[:, other, :], recv.at[7])
    pltpu.make_async_copy(cot_own, latent.at[:, mine, :], local.at[1]).wait()
    wait_bytes(out.at[:, 1 - core], recv.at[10])
    wait_bytes(out.at[:, core], send.at[13])
    wait_bytes(feat.at[pl.ds(0, NG - 1)], send.at[0])
    wait_bytes(feat.at[pl.ds(0, 48)], send.at[12])
    wait_bytes(lat_oth, send.at[1])
    wait_bytes(cot_oth, send.at[2])
    wait_bytes(op, send.at[3])
    wait_bytes(dop.at[pl.ds(0, ND - 1)], send.at[4])
    wait_bytes(dsec.at[pl.ds(0, NB - 1)], send.at[5])
    wait_bytes(cot_oth, send.at[7])
    wait_bytes(gband.at[pl.ds(0, 3)], send.at[8])
    wait_bytes(gq.at[pl.ds(0, 47)], send.at[9])
    wait_bytes(wg.at[pl.ds(0, 70)], send.at[6])
    wait_bytes(wg_s.at[pl.ds(0, 9)], send.at[11])
    wait_bytes(out.at[pl.ds(0, 31), core], send.at[10])

    @pl.when(head != quarter)
    def _():
        wait_bytes(feat.at[0], send.at[0])
        wait_bytes(dsec.at[0], send.at[5])

    @pl.when(me >= 48)
    def _():
        wait_bytes(gq.at[0], send.at[9])

    @pl.when(jnp.logical_or(me < 48, (me - 48) // 10 != col))
    def _():
        wait_bytes(wg_s.at[0], send.at[11])


VM = pl.BlockSpec(memory_space=pltpu.VMEM)
SM = pl.BlockSpec(memory_space=pltpu.SMEM)
ANY = pl.BlockSpec(memory_space=pl.ANY)


def struct(shape, dtype):
    return jax.ShapeDtypeStruct(shape, dtype)


def shards(spectrum, band_widths, band_weight, qkv_time, out_time, qkv_band, out_band, cotangent):
    tables = rotary_tables(np.arange(NP) * BP) + rotary_tables(np.arange(BP)) + rotary_tables(np.arange(256) // 8)
    tables = tuple(jnp.asarray(x) for x in tables)

    def vm(shape, dtype=BF):
        return pltpu.VMEM(shape, dtype)

    latent, out, share = pl.pallas_call(
        kernel,
        out_shape=[struct((NG, FB, D), BF), struct((32, 2, 32, D), BF), struct((48, 128), F32)],
        in_specs=[SM] + [ANY] * 13,
        out_specs=[ANY, ANY, VM],
        scratch_shapes=[
            vm((FB, 1280)), vm((D, 768)), vm((256, D)), vm((D, 768)), vm((256, D)),
            vm((NP, 128), F32), vm((NP, 128), F32), vm((BP, 128), F32), vm((BP, 128), F32),
            vm((256, 128), F32), vm((256, 128), F32),
            vm((T, T)), vm((BQ, T), F32), vm((NG, FB, W)), vm((NF, FB, W)), vm((NG, FB, D)),
            vm((NG, HF, D)), vm((NG, HF, D)), vm((NG, HF, D)), vm((D, 256)),
            vm((T, 128)), vm((T, 128)), vm((64, T)), vm((T, 128)), vm((128, T)),
            vm((T, 128), F32), vm((ND, 16, 128)), vm((ND, 16, 128)), vm((4, 256, 256)),
            vm((256, D), F32), vm((D, 768), F32), vm((256, D), F32),
            vm((NB, HF, D)), vm((ND, 16, 128)), vm((80, 16, D)),
            vm((ND, 16, 128)), vm((NB, HF, D)),
            vm((W, D)), vm((W, D), F32), vm((D, 256), F32), vm((4, 32, D)), vm((48, 16, 128)),
            vm((4, 32, D)), vm((32, D)), vm((ND, 16, 128)),
            pltpu.SemaphoreType.DMA((14,)), pltpu.SemaphoreType.DMA((12,)), pltpu.SemaphoreType.DMA((3,)),
            pltpu.SemaphoreType.DMA((4, 4)), pltpu.SemaphoreType.DMA((NQ,)), pltpu.SemaphoreType.DMA((8,)),
            pltpu.SemaphoreType.DMA((13,)),
            vm((8, 10, 16, D)), vm((10, 16, D)), vm((16, 16, D)),
            pltpu.SemaphoreType.REGULAR, pltpu.SemaphoreType.REGULAR,
        ],
        compiler_params=pltpu.CompilerParams(
            collective_id=1, has_side_effects=True, vmem_limit_bytes=VMEM_LIMIT
        ),
    )(band_widths, spectrum[0], band_weight.reshape(NG * W, D), qkv_time, out_time, qkv_band, out_band,
      cotangent[0], *tables)

    band_grad = out.reshape(NG, W, D).astype(F32)
    return (latent[None], band_grad, share.reshape(-1))


def solution(mesh):
    placed = (
        P(None, "frames", None),
        P(),
        P("bands", None, None),
        P(),
        P(),
        P(),
        P(),
        P(None, "bands", "frames", None),
    )
    return jax.shard_map(
        shards,
        mesh=mesh,
        in_specs=placed,
        out_specs=(
            P(None, "bands", "frames", None),
            P("bands", None, None),
            P(("frames", "bands")),
        ),
        check_vma=False,
    )
```

```python
import math

import jax
import jax.numpy as jnp
import numpy as np
from jax import lax
from jax.experimental import pallas as pl
from jax.experimental.pallas import tpu as pltpu
from jax.sharding import PartitionSpec as P

EPS = 1e-05
THETA = 10000.0
NB = 32
NG = 16
NF = 64
ND = 128
FB = 64
HF = 32
T = 4096
D = 384
W = 128
BQ = 256
NQ = T // BQ
BP = 512
NP = T // BP
CF = 512
CB = 1024
LOG2E = math.log2(math.e)
BF = jnp.bfloat16
F32 = jnp.float32
MESH = pl.DeviceIdType.MESH
VMEM_LIMIT = 63 * 1024 * 1024

NN = (((1,), (0,)), ((), ()))
NT = (((1,), (1,)), ((), ()))
TN = (((0,), (0,)), ((), ()))


def mm(a, b, dims=NN):
    return lax.dot_general(a, b, dims, preferred_element_type=F32)


def lanes(shape):
    return lax.broadcasted_iota(jnp.int32, shape, len(shape) - 1)


def swap_halves(x):
    lane = lanes(x.shape)
    ax = len(x.shape) - 1
    return jnp.where(lane % 64 < 32, pltpu.roll(x, 96, ax), pltpu.roll(x, 32, ax))


def rotary_tables(positions):
    i = np.arange(128) % 32
    freq = np.exp(i.astype(np.float64) * (-2.0 * math.log(THETA) / 64))
    sign = np.where(np.arange(128) % 64 < 32, -1.0, 1.0)
    ang = np.asarray(positions, np.float64)[:, None] * freq[None, :]
    return np.cos(ang).astype(np.float32), (np.sin(ang) * sign).astype(np.float32)


def here():
    return lax.axis_index("frames"), lax.axis_index("bands")


def wait_bytes(ref, sem):
    pltpu.make_async_copy(ref, ref, sem).wait()


def copy_to(src, dst, send_sem, recv_sem, frames, bands):
    pltpu.make_async_remote_copy(
        src, dst, send_sem, recv_sem, device_id=(frames, bands), device_id_type=MESH
    ).start()


def copy_out(src, dst, send_sem, recv_sem, frames, bands):
    fi, bi = here()
    mine = jnp.logical_and(frames == fi, bands == bi)

    @pl.when(mine)
    def _():
        pltpu.make_async_copy(src, dst, recv_sem).start()

    @pl.when(jnp.logical_not(mine))
    def _():
        copy_to(src, dst, send_sem, recv_sem, frames, bands)


def loop(lo, hi, body):
    def step(i, carry):
        body(i)
        return carry

    lax.fori_loop(lo, hi, step, 0)


def rows_of(j, n=BQ):
    return pl.ds(pl.multiple_of(j * n, n), n)


def angles_at(c, cc, sc, cr, sr):
    ca = cc[pl.ds(c, 1), :]
    sa = sc[pl.ds(c, 1), :]
    return ca * cr[...] - sa * sr[...], sa * cr[...] + ca * sr[...]


def normed_rows(feat_rows, bwk):
    lat = mm(feat_rows, bwk).astype(BF).astype(F32)
    r = lax.rsqrt(jnp.mean(lat * lat, axis=-1, keepdims=True) + EPS)
    return lat * r, r


def own_columns(qt, wh):
    head = lax.rem(lax.axis_index("frames"), 4)
    parts = []
    for s in range(3):
        x = qt[:, pl.ds(pl.multiple_of(s * 256 + (head // 2) * 128, 128), 128)].astype(F32)
        parts.append(jnp.where(lax.rem(head, 2) == 1, pltpu.roll(x, 64, 1), x))
    low = lanes((D, 128)) < 64
    wh[:, 0:128] = jnp.where(low, parts[0], pltpu.roll(parts[1], 64, 1)).astype(BF)
    wh[:, 128:256] = jnp.where(low, parts[2], 0.0).astype(BF)


def make_features(widths, spec, bw, feat, lat):
    bi = lax.axis_index("bands")
    start = jnp.int32(0)
    for j in range(NG):
        start = start + jnp.where(bi == 1, widths[j], 0)

    lane = lanes((256, W))
    diff = lax.broadcasted_iota(jnp.int32, (256, W), 0) - lane

    def one(k, start):
        w = widths[bi * NG + k]
        blk = (2 * start) // 128
        a = spec[:, 0:128]
        b = spec[:, 128:256]
        last = spec.shape[1] // 128 - 1
        for n in range(1, last + 1):
            a = jnp.where(blk == n, spec[:, 128 * n:128 * n + 128], a)
        for n in range(2, last + 1):
            b = jnp.where(blk == n - 1, spec[:, 128 * n:128 * n + 128], b)
        pick = jnp.logical_and(diff == 2 * start - 128 * blk, lane < 2 * w)
        y = mm(jnp.concatenate([a, b], axis=1), jnp.where(pick, 1.0, 0.0).astype(BF)).astype(BF)
        feat[k] = y
        lat[k] = mm(y, bw[rows_of(k, W), 0:D]).astype(BF)
        return start + w

    lax.fori_loop(0, NG, one, start)


def project(feat, step, bwk, wh, tables, q_s, k_s, kt_s, v_s, vt_s):
    def pre(j):
        rows = rows_of(j, BP)
        f = feat[rows_of(j, 8)].reshape(BP, W)
        n, _r = normed_rows(f, bwk[...])
        proj = mm(n.astype(BF), wh[...])
        co, si = angles_at(j, *tables)
        a = proj[:, :128]
        a = a * co + swap_halves(a) * si
        low = lanes(a.shape) < 64
        q_s[rows, :] = (a * (0.125 * LOG2E)).astype(BF)
        k = jnp.where(low, pltpu.roll(a, 64, 1), 0.0)
        k_s[rows, :] = k.astype(BF)
        kt_s[:, rows] = k.T[:64].astype(BF)
        v = jnp.where(low, proj[:, 128:], 1.0)
        v_s[rows, :] = v.astype(BF)
        vt_s[:, rows] = v.T.astype(BF)

    def quarter(i):
        at = step(i)
        loop(0, 2, lambda u: pre(2 * at + u))

    loop(0, 4, quarter)


def attend(blk, q_s, kt_s, v_s, e_s, s_s, ol, op):
    rows = rows_of(blk)
    q = q_s[rows, :][:, :64]
    top = jnp.full((BQ, 128), -jnp.inf, F32)
    for j in range(T // CF):
        cols = slice(j * CF, (j + 1) * CF)
        s = mm(q, kt_s[:, cols])
        s_s[:, cols] = s
        for i in range(CF // 128):
            top = jnp.maximum(top, s[:, 128 * i:128 * i + 128])
    top = jnp.max(top, axis=1, keepdims=True)
    res = jnp.zeros((BQ, 128), F32)
    for j in range(T // CF):
        cols = slice(j * CF, (j + 1) * CF)
        e = jnp.exp2(s_s[:, cols] - top).astype(BF)
        e_s[rows, cols] = e
        res = res + mm(e, v_s[cols, :])
    rl = 1.0 / res
    low = lanes(res.shape) < 64
    o = res * pltpu.roll(rl, 64, 1)
    ol[rows, :] = jnp.where(low, o, rl)
    o4 = o.reshape(BQ // HF, 2, 16, 128)
    low3 = lanes((BQ // HF, 16, 128)) < 64
    op[pl.ds(pl.multiple_of(blk * 8, 8), 8)] = jnp.where(low3, o4[:, 0], pltpu.roll(o4[:, 1], 64, 2)).astype(BF)


def attend_back(c, e_s, q_s, k_s, vt_s, ol, dop, t_s):
    rows = rows_of(c)
    x = dop[pl.ds(pl.multiple_of(c * 8, 8), 8)].astype(F32)
    do = jnp.concatenate([x[:, None], pltpu.roll(x, 64, 2)[:, None]], axis=1).reshape(BQ, 128)
    o = ol[rows, :]
    lane = lanes((BQ, 128))
    do = jnp.where(lane < 64, do * pltpu.roll(o, 64, 1), 0.0)
    delta = jnp.sum(do * o, axis=1, keepdims=True)
    hi = delta.astype(BF).astype(F32)
    aug = jnp.where(lane == 64, -hi, jnp.where(lane == 65, hi - delta, do)).astype(BF)
    do_t = do.T[:64].astype(BF)
    q_t = q_s[rows, :].astype(F32).T[:64].astype(BF)
    dq = jnp.zeros((BQ, 128), F32)
    for j in range(T // CB):
        cols = slice(j * CB, (j + 1) * CB)
        e = e_s[rows, cols]
        ds = (e.astype(F32) * mm(aug, vt_s[:, cols])).astype(BF)
        dq = dq + mm(ds, k_s[cols, :])
        t_s[0:64, cols] += mm(do_t, e)
        t_s[64:128, cols] += mm(q_t, ds)
    ol[rows, :] = dq * 0.125


def project_back(feat, bwk, wh, tables, dq_s, t_s, gb_s, dproj_s, n_s):
    low = lanes((BP, 128)) < 64

    def post(j):
        rows = rows_of(j, BP)
        tx = t_s[0:128, rows].T
        a = jnp.where(low, dq_s[rows, :], tx * math.log(2.0)).astype(BF).astype(F32)
        co, si = angles_at(j, *tables)
        a = a * co - swap_halves(a) * si
        dproj = jnp.concatenate([a, jnp.where(low, tx, 0.0)], axis=1).astype(BF)
        dn = mm(dproj, wh[...], NT).astype(BF).astype(F32)
        f = feat[rows_of(j, 8)].reshape(BP, W)
        n, r = normed_rows(f, bwk[...])
        dlat = (r * (dn - n * jnp.mean(n * dn, axis=1, keepdims=True))).astype(BF)
        gb_s[...] += mm(f, dlat, TN)
        dproj_s[rows, :] = dproj
        n_s[rows, :] = n.astype(BF)

    loop(0, NP, post)


def band_layer(lat_all, lat_oth, cot_own, cot_oth, att, w_ot, w_qb, w_ob, cb, sb,
               lat_keep, lat_send, dsec_out, dop_out, wg_out, s_s, att_s, g_ot, g_qb, g_ob, wait_att):
    bi = lax.axis_index("bands")
    own = pl.ds(pl.multiple_of(bi * 128, 128), 128)
    oth = pl.ds(pl.multiple_of((1 - bi) * 128, 128), 128)
    mine = pl.ds(pl.multiple_of(bi * HF, HF), HF)

    def lat_at(g):
        return pl.ds(pl.multiple_of(g * D, 128), D)

    def cot_at(g):
        return pl.ds(pl.multiple_of(4 * D + g * D, 128), D)

    def do_at(g):
        return pl.ds(pl.multiple_of(8 * D + g * 256, 128), 256)

    for x, at, where in ((lat_all[:, mine, :], lat_at, own), (lat_oth[...], lat_at, oth),
                         (cot_own[...], cot_at, own), (cot_oth[...], cot_at, oth)):
        x = x.astype(F32)
        for g in range(4):
            s_s[where, at(g)] = x[:, 8 * g:8 * g + 8, :].reshape(128, D)
    g_ot[...] = jnp.zeros_like(g_ot)
    g_qb[...] = jnp.zeros_like(g_qb)
    g_ob[...] = jnp.zeros_like(g_ob)
    low = lanes((256, 128)) < 64
    wait_att()

    def pair(a, b, p):
        if p == 0:
            return jnp.where(low, a, pltpu.roll(b, 64, 1))
        return jnp.where(low, pltpu.roll(a, 64, 1), b)

    for j in range(2):
        x0 = att[:, 2 * j].astype(F32)
        x1 = att[:, 2 * j + 1].astype(F32)
        for g in range(4):
            p, rr = g // 2, g % 2
            a = x0[:, 8 * rr:8 * rr + 8, :].reshape(256, 128)
            b = x1[:, 8 * rr:8 * rr + 8, :].reshape(256, 128)
            att_s[g, :, 128 * j:128 * j + 128] = pair(a, b, p).astype(BF)

    def group(g):
        att_g = att_s[g]
        cot = s_s[:, cot_at(g)]
        cot_b = cot.astype(BF)
        sec = (s_s[:, lat_at(g)] + mm(att_g, w_ot[...])).astype(BF).astype(F32)
        r = lax.rsqrt(jnp.mean(sec * sec, axis=-1, keepdims=True) + EPS)
        n = sec * r
        nb = n.astype(BF)
        proj = mm(nb, w_qb[...])
        dbatt = mm(cot_b, w_ob[...], NT)
        co, si = cb[...], sb[...]
        row_t = lax.broadcasted_iota(jnp.int32, (256, 256), 0) % 8
        col_t = lax.broadcasted_iota(jnp.int32, (256, 256), 1) % 8
        same = row_t == col_t
        batts, dqs, dks, dvs = [], [], [], []
        for j in range(2):
            q = proj[:, 128 * j:128 * j + 128]
            k = proj[:, 256 + 128 * j:384 + 128 * j]
            v = proj[:, 512 + 128 * j:640 + 128 * j].astype(BF)
            q = ((q * co + swap_halves(q) * si) * 0.125).astype(BF)
            k = (k * co + swap_halves(k) * si).astype(BF)
            do = dbatt[:, 128 * j:128 * j + 128].astype(BF)
            outs = []
            for hh in range(2):
                part = low if hh == 0 else jnp.logical_not(low)
                zero = jnp.zeros((), BF)
                qm = jnp.where(part, q, zero)
                dm = jnp.where(part, do, zero)
                s = jnp.where(same, mm(qm, k, NT), -jnp.inf)
                e = jnp.exp(s - jnp.max(s, axis=1, keepdims=True))
                p = e * (1.0 / jnp.sum(e, axis=1, keepdims=True))
                pb = p.astype(BF)
                pf = pb.astype(F32)
                o = mm(pb, v)
                dp = mm(dm, v, NT)
                ds = (pf * (dp - jnp.sum(pf * dp, axis=1, keepdims=True))).astype(BF)
                outs.append((o, mm(ds, k), mm(ds, q, TN), mm(pb, do, TN)))
            batts.append(jnp.where(low, outs[0][0], outs[1][0]).astype(BF))
            dq = (jnp.where(low, outs[0][1], outs[1][1]) * 0.125).astype(BF).astype(F32)
            dk = jnp.where(low, outs[0][2], outs[1][2]).astype(BF).astype(F32)
            dqs.append((dq * co - swap_halves(dq) * si).astype(BF))
            dks.append((dk * co - swap_halves(dk) * si).astype(BF))
            dvs.append(jnp.where(low, outs[0][3], outs[1][3]).astype(BF))
        batt = jnp.concatenate(batts, axis=1)
        dproj = jnp.concatenate(dqs + dks + dvs, axis=1)
        s_s[:, lat_at(g)] = sec + mm(batt, w_ob[...])
        dn = mm(dproj, w_qb[...], NT).astype(BF).astype(F32)
        dsec = (cot + r * (dn - n * jnp.mean(n * dn, axis=1, keepdims=True))).astype(BF)
        s_s[:, cot_at(g)] = dsec.astype(F32)
        s_s[:, do_at(g)] = mm(dsec, w_ot[...], NT)
        g_ob[...] += mm(batt, cot_b, TN)
        g_qb[...] += mm(nb, dproj, TN)
        g_ot[...] += mm(att_g, dsec, TN)

    loop(0, 4, group)

    for j in range(2):
        for hh in range(2):
            parts = []
            for rr in range(2):
                a = s_s[:, do_at(rr)][:, 128 * j:128 * j + 128]
                b = s_s[:, do_at(2 + rr)][:, 128 * j:128 * j + 128]
                parts.append(pair(a, b, hh).reshape(NB, 8, 128))
            dop_out[:, 2 * j + hh] = jnp.concatenate(parts, axis=1).astype(BF)

    def rest():
        dsec_out[...] = jnp.concatenate(
            [s_s[:, cot_at(g)].reshape(NB, 8, D) for g in range(4)], axis=1
        ).astype(BF)
        for ref, where in ((lat_keep, own), (lat_send, oth)):
            ref[...] = jnp.concatenate(
                [s_s[where, lat_at(g)].reshape(NG, 8, D) for g in range(4)], axis=1
            ).astype(BF)
        wg_out[0:16] = g_ot[...].reshape(16, 16, D).astype(BF)
        wg_out[16:64] = jnp.concatenate(
            [g_qb[:, :D].reshape(48, 8, D), g_qb[:, D:].reshape(48, 8, D)], axis=1
        ).astype(BF)
        wg_out[64:80] = g_ob[...].reshape(16, 16, D).astype(BF)

    return rest


def kernel(widths, spec_h, bw, qt_h, w_ot_h, w_qb_h, w_ob_h, cot, cc_h, sc_h, cr_h, sr_h, cb_h, sb_h,
           latent, out, share,
           spec, qt, w_ot, w_qb, w_ob, cc, sc, cr, sr, cb, sb,
           e_s, s_s, feat_own, feat, lat_all, lat_oth, cot_own, cot_oth, wh, q_s, k_s, kt_s, v_s, vt_s,
           ol, op, att, att_s, g_ot, g_qb, g_ob, dsec, dop, wg, dop_r, dsec_r,
           bwk, gb_s, gq_s, gband, gq, quad, part, gq_r, send, recv, local,
           feat_in, dop_in, out_in, staged,
           wg_p, wg_s, wg_r, rows_in, group_in):
    fi, bi = here()
    me = fi * 2 + bi
    slot = bi * NF + fi
    head = lax.rem(fi, 4)
    tables = (cc, sc, cr, sr)
    mine = pl.ds(pl.multiple_of(bi * HF, HF), HF)
    other = pl.ds(pl.multiple_of((1 - bi) * HF, HF), HF)

    barrier = pltpu.get_barrier_semaphore()

    row, col = fi // 8, lax.rem(fi, 8)

    def greet(d):
        in_row = row * 8 + lax.rem(col + d, 8)
        in_col = lax.rem(row + d, 8) * 8 + col
        pl.semaphore_signal(barrier, inc=1, device_id=(in_row, bi), device_id_type=MESH)
        pl.semaphore_signal(barrier, inc=1, device_id=(in_col, bi), device_id_type=MESH)

    loop(1, 8, greet)
    pl.semaphore_signal(barrier, inc=1, device_id=(fi, 1 - bi), device_id_type=MESH)

    bw_at = e_s.at[pl.ds(0, NG * W), pl.ds(0, D)]
    first = ((bw, bw_at), (spec_h, spec), (qt_h, qt))
    later = ((cc_h, cc), (sc_h, sc), (cr_h, cr), (sr_h, sr), (w_ot_h, w_ot), (w_qb_h, w_qb), (w_ob_h, w_ob),
             (cb_h, cb), (sb_h, sb), (cot.at[:, mine, :], cot_own))
    copies = [pltpu.make_async_copy(x, y, staged.at[i]) for i, (x, y) in enumerate(first + later)]
    for c in copies:
        c.start()
    pl.semaphore_wait(barrier, 15)

    def greet_again(d):
        in_col = lax.rem(row + d, 8) * 8 + col
        pl.semaphore_signal(rows_in, inc=1, device_id=(in_col, bi), device_id_type=MESH)

    loop(1, 8, greet_again)
    for c in copies[:len(first)]:
        c.wait()
    own_columns(qt, wh)
    make_features(widths, spec, e_s, feat_own, lat_all)
    bwk[...] = e_s[rows_of(fi // 4, W), 0:D]
    for c in copies[len(first):]:
        c.wait()
    pl.semaphore_wait(rows_in, 7)
    pl.semaphore_signal(group_in, inc=1, device_id=(fi, 1 - bi), device_id_type=MESH)

    quarter = fi // 16

    def give_features(d):
        k = lax.rem(fi + d, NG)
        copy_out(feat_own.at[k], feat.at[fi], send.at[0], feat_in.at[0, lax.rem(fi, 16) // 4], 4 * k + quarter, bi)

    loop(0, NG, give_features)
    mate = fi + 1 - 2 * lax.rem(fi, 2)
    near = fi + 2 - 4 * lax.rem(fi // 2, 2)

    def give_halves():
        copy_to(cot.at[:, other, :], cot_oth, send.at[2], recv.at[2], fi, 1 - bi)
        copy_to(lat_all.at[:, other, :], lat_oth, send.at[1], recv.at[1], fi, 1 - bi)

    def part_of(quarter, q):
        return feat.at[pl.ds(pl.multiple_of(quarter * 16 + q * 4, 4), 4)]

    def spread(q):
        block = part_of(head, q)
        wait_bytes(block, feat_in.at[0, q])
        copy_to(block, block, send.at[12], feat_in.at[1, q], mate, bi)
        copy_to(block, block, send.at[12], feat_in.at[2, q], near, bi)

    loop(0, 4, spread)

    def step(i):
        at = 2 * lax.rem(head // 2 + i // 2, 2) + lax.rem(head + i, 2)

        @pl.when(i == 1)
        def _():
            give_halves()

        @pl.when(i == 2)
        def _():
            def forward_on(q):
                block = part_of(at, q)
                wait_bytes(block, feat_in.at[2, q])
                copy_to(block, block, send.at[12], feat_in.at[3, q], mate, bi)

            loop(0, 4, forward_on)

        @pl.when(lax.rem(i, 2) == 1)
        def _():
            loop(0, 4, lambda q: wait_bytes(part_of(at, q), feat_in.at[i, q]))

        return at

    project(feat, step, bwk, wh, tables, q_s, k_s, kt_s, v_s, vt_s)
    pl.semaphore_wait(group_in, 1)

    def give_block(blk):
        for u in range(8):
            d = blk * 8 + u
            self_here = d == me
            copy_to(op.at[d], att.at[jnp.where(self_here, (1 - bi) * NF + fi, slot)], send.at[3], recv.at[3],
                    jnp.where(self_here, fi, d // 2), jnp.where(self_here, 1 - bi, lax.rem(d, 2)))

    first_blk = fi // 4
    attend(first_blk, q_s, kt_s, v_s, e_s, s_s, ol, op)

    def forward(c):
        give_block(lax.rem(c + first_blk + NQ - 1, NQ))
        attend(lax.rem(c + first_blk, NQ), q_s, kt_s, v_s, e_s, s_s, ol, op)

    loop(1, NQ, forward)
    give_block(lax.rem(first_blk + NQ - 1, NQ))

    def wait_att():
        wait_bytes(att, recv.at[3])
        att[slot] = op[me]

    wait_bytes(lat_oth, recv.at[1])
    wait_bytes(cot_oth, recv.at[2])
    rest = band_layer(
        lat_all, lat_oth, cot_own, cot_oth, att.reshape(NB, 4, 16, 128), w_ot, w_qb, w_ob, cb, sb,
        cot_own, cot_oth, dsec, dop.reshape(NB, 4, 16, 128), wg, s_s, att_s, g_ot, g_qb, g_ob,
        wait_att)

    group = fi // 4
    pltpu.make_async_copy(dop.at[slot], dop_r.at[me], dop_in.at[group]).start()
    copy_to(dop.at[(1 - bi) * NF + fi], dop_r.at[me], send.at[4], dop_in.at[group], fi, 1 - bi)

    def give_back(d):
        f = lax.rem(fi + d, NF)
        copy_to(dop.at[f], dop_r.at[me], send.at[4], dop_in.at[group], f, 0)
        copy_to(dop.at[NF + f], dop_r.at[me], send.at[4], dop_in.at[group], f, 1)

    def give_some(n):
        for u in range(7):
            give_back(1 + 7 * n + u)

    loop(0, 9, give_some)
    rest()

    place = lax.rem(fi, 16) * 2 + bi

    def give_second():
        def one(k):
            copy_out(dsec.at[k], dsec_r.at[place], send.at[5], recv.at[5],
                     lax.rem(k, NG) * 4 + quarter, k // NG)

        loop(0, NB, one)

    def give_latent():
        copy_to(cot_oth, latent.at[:, mine, :], send.at[7], recv.at[7], fi, 1 - bi)
        pltpu.make_async_copy(cot_own, latent.at[:, mine, :], local.at[1]).start()

    def give_weights():
        pltpu.make_async_copy(wg.at[rows_of(col, 10)], wg_p.at[col], recv.at[6]).start()

        def one(d):
            t = lax.rem(col + d, 8)
            copy_to(wg.at[rows_of(t, 10)], wg_p.at[col], send.at[6], recv.at[6], row * 8 + t, bi)

        loop(1, 8, one)

    def give_sums():
        wait_bytes(wg_p, recv.at[6])
        wg_s[...] = jnp.sum(wg_p[...].astype(F32), axis=0).astype(BF)

        def one(u):
            d = 48 + col * 10 + u
            copy_out(wg_s.at[u], wg_r.at[row * 2 + bi], send.at[11], recv.at[11], d // 2, lax.rem(d, 2))

        loop(0, 10, one)

    s_s[0:128, :] = jnp.zeros((128, T), F32)

    def backward(i):
        c = lax.rem(group + 2 * NQ - 1 - i, NQ)
        wait_bytes(dop_r.at[rows_of(c, 8)], dop_in.at[c])
        attend_back(c, e_s, q_s, k_s, vt_s, ol, dop_r, s_s)
        pl.when(i == 3)(give_second)
        pl.when(i == 5)(give_weights)
        pl.when(i == 7)(give_latent)
        pl.when(i == 13)(give_sums)

    loop(0, NQ, backward)

    wait_bytes(dsec_r, recv.at[5])
    f = feat[rows_of(head, 16)].reshape(1024, W)
    gb_s[...] = mm(f, dsec_r[...].reshape(1024, D), TN)
    dproj_s = e_s.at[:, pl.ds(0, 256)]
    n_s = e_s.at[:, pl.ds(256, D)]
    project_back(feat, bwk, wh, tables, ol, s_s, gb_s, dproj_s, n_s)

    gband[...] = gb_s[...].reshape(4, 32, D).astype(BF)
    base = fi - head
    pltpu.make_async_copy(gband.at[head], quad.at[head], recv.at[8]).start()
    for d in range(1, 4):
        t = lax.rem(head + d, 4)
        copy_to(gband.at[t], quad.at[head], send.at[8], recv.at[8], base + t, bi)

    gq_s[...] = jnp.zeros_like(gq_s)

    def weight(j):
        rows = rows_of(j, 1024)
        gq_s[...] += mm(n_s[rows, :], dproj_s[rows, :], TN)

    loop(0, 4, weight)

    chip, core = fi // 2, lax.rem(fi, 2)
    wait_bytes(quad, recv.at[8])
    part[...] = jnp.sum(quad[...].astype(F32), axis=0).astype(BF)
    pltpu.make_async_copy(part, out.at[chip, core], out_in.at[chip // 4]).start()

    def give_band(d):
        copy_to(part, out.at[chip, core], send.at[10], out_in.at[chip // 4],
                lax.rem(chip + d, 32) * 2 + core, bi)

    loop(1, 32, give_band)

    g = gq_s[...]
    gq[...] = jnp.concatenate(
        [g[:, :128].reshape(48, 8, 128), g[:, 128:].reshape(48, 8, 128)], axis=1
    ).astype(BF)
    loop(0, 48, lambda d: copy_out(gq.at[d], gq_r.at[me], send.at[9], recv.at[9], d // 2, lax.rem(d, 2)))

    def pass_on(i):
        j = lax.rem(chip // 4 + 15 - i, 8)
        block = out.at[rows_of(j, 4), core]
        wait_bytes(block, out_in.at[j])
        copy_to(block, block, send.at[13], recv.at[10], mate, bi)

    low8 = lanes((8, 128)) < 64

    loop(0, 8, pass_on)

    @pl.when(me < 48)
    def _():
        wait_bytes(gq_r, recv.at[9])
        x = jnp.sum(gq_r[...].reshape(NG, 4, 2, 16, 128).astype(F32), axis=(0, 2))
        for j in range(2):
            a, b = x[2 * j], x[2 * j + 1]
            share[pl.ds(j, 8, stride=6), :] = jnp.where(low8, a[:8], pltpu.roll(b[:8], 64, 1))
            share[pl.ds(2 + j, 8, stride=6), :] = jnp.where(low8, pltpu.roll(a[:8], 64, 1), b[:8])
            share[pl.ds(4 + j, 8, stride=6), :] = jnp.where(low8, a[8:], pltpu.roll(b[8:], 64, 1))

    @pl.when(me >= 48)
    def _():
        wait_bytes(wg_r, recv.at[11])
        x = jnp.sum(wg_r[...].astype(F32), axis=0)
        wide = jnp.logical_and(me >= 64, me < 112)

        @pl.when(wide)
        def _():
            for j in range(3):
                share[pl.ds(j, 8, stride=6), :] = x[:8, 128 * j:128 * j + 128]
                share[pl.ds(3 + j, 8, stride=6), :] = x[8:, 128 * j:128 * j + 128]

        @pl.when(jnp.logical_not(wide))
        def _():
            for j in range(3):
                share[pl.ds(j, 16, stride=3), :] = x[:, 128 * j:128 * j + 128]

    wait_bytes(latent.at[:, other, :], recv.at[7])
    pltpu.make_async_copy(cot_own, latent.at[:, mine, :], local.at[1]).wait()
    wait_bytes(out.at[:, 1 - core], recv.at[10])
    wait_bytes(out.at[:, core], send.at[13])
    wait_bytes(feat.at[pl.ds(0, NG - 1)], send.at[0])
    wait_bytes(feat.at[pl.ds(0, 48)], send.at[12])
    wait_bytes(lat_oth, send.at[1])
    wait_bytes(cot_oth, send.at[2])
    wait_bytes(op, send.at[3])
    wait_bytes(dop.at[pl.ds(0, ND - 1)], send.at[4])
    wait_bytes(dsec.at[pl.ds(0, NB - 1)], send.at[5])
    wait_bytes(cot_oth, send.at[7])
    wait_bytes(gband.at[pl.ds(0, 3)], send.at[8])
    wait_bytes(gq.at[pl.ds(0, 47)], send.at[9])
    wait_bytes(wg.at[pl.ds(0, 70)], send.at[6])
    wait_bytes(wg_s.at[pl.ds(0, 9)], send.at[11])
    wait_bytes(out.at[pl.ds(0, 31), core], send.at[10])

    @pl.when(head != quarter)
    def _():
        wait_bytes(feat.at[0], send.at[0])
        wait_bytes(dsec.at[0], send.at[5])

    @pl.when(me >= 48)
    def _():
        wait_bytes(gq.at[0], send.at[9])

    @pl.when(jnp.logical_or(me < 48, (me - 48) // 10 != col))
    def _():
        wait_bytes(wg_s.at[0], send.at[11])


VM = pl.BlockSpec(memory_space=pltpu.VMEM)
SM = pl.BlockSpec(memory_space=pltpu.SMEM)
ANY = pl.BlockSpec(memory_space=pl.ANY)


def struct(shape, dtype):
    return jax.ShapeDtypeStruct(shape, dtype)


def shards(spectrum, band_widths, band_weight, qkv_time, out_time, qkv_band, out_band, cotangent):
    tables = rotary_tables(np.arange(NP) * BP) + rotary_tables(np.arange(BP)) + rotary_tables(np.arange(256) // 8)
    tables = tuple(jnp.asarray(x) for x in tables)

    def vm(shape, dtype=BF):
        return pltpu.VMEM(shape, dtype)

    latent, out, share = pl.pallas_call(
        kernel,
        out_shape=[struct((NG, FB, D), BF), struct((32, 2, 32, D), BF), struct((48, 128), F32)],
        in_specs=[SM] + [ANY] * 13,
        out_specs=[ANY, ANY, VM],
        scratch_shapes=[
            vm((FB, 1280)), vm((D, 768)), vm((256, D)), vm((D, 768)), vm((256, D)),
            vm((NP, 128), F32), vm((NP, 128), F32), vm((BP, 128), F32), vm((BP, 128), F32),
            vm((256, 128), F32), vm((256, 128), F32),
            vm((T, T)), vm((BQ, T), F32), vm((NG, FB, W)), vm((NF, FB, W)), vm((NG, FB, D)),
            vm((NG, HF, D)), vm((NG, HF, D)), vm((NG, HF, D)), vm((D, 256)),
            vm((T, 128)), vm((T, 128)), vm((64, T)), vm((T, 128)), vm((128, T)),
            vm((T, 128), F32), vm((ND, 16, 128)), vm((ND, 16, 128)), vm((4, 256, 256)),
            vm((256, D), F32), vm((D, 768), F32), vm((256, D), F32),
            vm((NB, HF, D)), vm((ND, 16, 128)), vm((80, 16, D)),
            vm((ND, 16, 128)), vm((NB, HF, D)),
            vm((W, D)), vm((W, D), F32), vm((D, 256), F32), vm((4, 32, D)), vm((48, 16, 128)),
            vm((4, 32, D)), vm((32, D)), vm((ND, 16, 128)),
            pltpu.SemaphoreType.DMA((14,)), pltpu.SemaphoreType.DMA((12,)), pltpu.SemaphoreType.DMA((3,)),
            pltpu.SemaphoreType.DMA((4, 4)), pltpu.SemaphoreType.DMA((NQ,)), pltpu.SemaphoreType.DMA((8,)),
            pltpu.SemaphoreType.DMA((13,)),
            vm((8, 10, 16, D)), vm((10, 16, D)), vm((16, 16, D)),
            pltpu.SemaphoreType.REGULAR, pltpu.SemaphoreType.REGULAR,
        ],
        compiler_params=pltpu.CompilerParams(
            collective_id=1, has_side_effects=True, vmem_limit_bytes=VMEM_LIMIT
        ),
    )(band_widths, spectrum[0], band_weight.reshape(NG * W, D), qkv_time, out_time, qkv_band, out_band,
      cotangent[0], *tables)

    band_grad = out.reshape(NG, W, D).astype(F32)
    return (latent[None], band_grad, share.reshape(-1))


def solution(mesh):
    placed = (
        P(None, "frames", None),
        P(),
        P("bands", None, None),
        P(),
        P(),
        P(),
        P(),
        P(None, "bands", "frames", None),
    )
    return jax.shard_map(
        shards,
        mesh=mesh,
        in_specs=placed,
        out_specs=(
            P(None, "bands", "frames", None),
            P("bands", None, None),
            P(("frames", "bands")),
        ),
        check_vma=False,
    )
```
